512 devices in a mesh: batch: 64 (over z, y_lo, core), tensor: 8 (over x, y_hi).
Axes of the slice: x: 4, y: 4 (y_hi: 2, y_lo: 2; y = y_hi * 2 + y_lo), z: 16, core: 2. Of those that a mesh axis runs over, the one named last changes fastest.
Arguments:
- image_student: bfloat16 [12288, 512], P('batch', 'tensor'), may hold values from -64 to 64
- text_student: bfloat16 [12288, 512], P(('batch', 'tensor')), may hold values from -4 to 4
- image_teacher: bfloat16 [12288, 1280], P('batch'), may hold values from -64 to 64
- text_teacher: bfloat16 [12288, 1280], P(('batch', 'tensor')), may hold values from -4 to 4
- student_scale: float32 [1], replicated, may hold values from 1.5 to 3
- teacher_scale: float32 [1], replicated, may hold values from 1.5 to 3
Outputs:
- pair_loss: float32 [12288], P(('batch', 'tensor'))
- grad_image: float32 [12288, 512], P('batch', 'tensor')
- grad_text: float32 [12288, 512], P(('batch', 'tensor'))
The draws below stay inside these ranges and needn't reach their ends.
All inputs are finite; a program needn't handle non-finite values.
Results may differ from the reference program's by a relative error of at most 0.0065.
Values may be sent and summed in bfloat16 or wider, within the bound.
A program may use at most 64 MiB of HBM per device.

```python
import math
import jax
import jax.numpy as jnp
from jax import lax

DS = 512
DT = 1280
BATCH = 12288


def text_rows(key, salt, width):
    return jax.random.truncated_normal(jax.random.fold_in(key, salt), -4.0, 4.0, (BATCH, width), jnp.float32)


def draw_image_student(key, part):
    key = jax.random.fold_in(key, 21)
    images = jax.random.truncated_normal(key, -4.0, 4.0, (BATCH, DS), jnp.float32)
    return images.astype(jnp.bfloat16)


def draw_text_student(key, part):
    return text_rows(key, 11, DS).astype(jnp.bfloat16)


def draw_image_teacher(key, part):
    key = jax.random.fold_in(key, 22)
    images = jax.random.truncated_normal(key, -4.0, 4.0, (BATCH, DT), jnp.float32)
    return images.astype(jnp.bfloat16)


def draw_text_teacher(key, part):
    return text_rows(key, 12, DT).astype(jnp.bfloat16)


def setup_inputs(seed: int = 0) -> dict:
    splits = jax.random.split(jax.random.key(seed), 7)
    return {
        "image_student": draw_image_student(jax.random.fold_in(splits[6], 71), 0),
        "text_student": draw_text_student(jax.random.fold_in(splits[6], 71), 0),
        "image_teacher": draw_image_teacher(jax.random.fold_in(splits[6], 71), 0),
        "text_teacher": draw_text_teacher(jax.random.fold_in(splits[6], 71), 0),
        "student_scale": jnp.clip(jnp.exp(jax.random.uniform(splits[4], (1,), jnp.float32, math.log(1.5), math.log(3.0))), 1.5, 3.0),
        "teacher_scale": jnp.clip(jnp.exp(jax.random.uniform(splits[5], (1,), jnp.float32, math.log(1.5), math.log(3.0))), 1.5, 3.0),
    }


def tile_scores(image_block, teacher_block, text_student, text_teacher, factors):
    student = jnp.dot(image_block, text_student.T, preferred_element_type=jnp.float32) * factors[0]
    teacher = jnp.dot(teacher_block, text_teacher.T, preferred_element_type=jnp.float32) * factors[1]
    return (student, teacher)

def reference(image_student, text_student, image_teacher, text_teacher, student_scale, teacher_scale):
    factors = (student_scale[0] / jnp.sqrt(jnp.float32(DS)), teacher_scale[0] / jnp.sqrt(jnp.float32(DT)))
    height = math.gcd(BATCH, 512)
    number = BATCH // height
    image_blocks = image_student.reshape(number, height, DS)
    teacher_blocks = image_teacher.reshape(number, height, DT)

    def first_pass(carry, blocks):
        col_peak, col_sums, col_weighted = carry
        student, teacher = tile_scores(blocks[0], blocks[1], text_student, text_teacher, factors)
        row_peak = jnp.stack([lax.optimization_barrier(jnp.max(student, 1)), lax.optimization_barrier(jnp.max(teacher, 1))])
        teacher_rows = jnp.exp(teacher - row_peak[1][:, None])
        row_sums = jnp.stack([lax.optimization_barrier(jnp.sum(jnp.exp(student - row_peak[0][:, None]), 1)), lax.optimization_barrier(jnp.sum(teacher_rows, 1))])
        row_weighted = lax.optimization_barrier(jnp.sum(teacher_rows * student, 1))
        block_peak = jnp.stack([lax.optimization_barrier(jnp.max(student, 0)), lax.optimization_barrier(jnp.max(teacher, 0))])
        peak = jnp.maximum(col_peak, block_peak)
        teacher_cols = jnp.exp(teacher - peak[1][None, :])
        rescale = jnp.exp(col_peak - peak)
        sums = col_sums * rescale + jnp.stack([lax.optimization_barrier(jnp.sum(jnp.exp(student - peak[0][None, :]), 0)), lax.optimization_barrier(jnp.sum(teacher_cols, 0))])
        weighted = col_weighted * rescale[1] + lax.optimization_barrier(jnp.sum(teacher_cols * student, 0))
        return ((peak, sums, weighted), (row_peak, row_sums, row_weighted))
    start_carry = (jnp.full((2, BATCH), -jnp.inf, jnp.float32), jnp.zeros((2, BATCH), jnp.float32), jnp.zeros((BATCH,), jnp.float32))
    col_stats, row_parts = lax.scan(first_pass, start_carry, (image_blocks, teacher_blocks))
    row_peak = jnp.moveaxis(row_parts[0], 0, 1).reshape(2, BATCH)
    row_sums = jnp.moveaxis(row_parts[1], 0, 1).reshape(2, BATCH)
    row_weighted = row_parts[2].reshape(BATCH)
    row_lse = row_peak + jnp.log(row_sums)
    col_lse = col_stats[0] + jnp.log(col_stats[1])
    row_loss = row_lse[0] - row_weighted / row_sums[1]
    col_loss = col_lse[0] - col_stats[2] / col_stats[1][1]
    pair_loss = 0.5 * (row_loss + col_loss)
    row_lse_blocks = jnp.moveaxis(row_lse.reshape(2, number, height), 1, 0)

    def second_pass(text_grad, blocks):
        image_block, teacher_block, lse_block = blocks
        student, teacher = tile_scores(image_block, teacher_block, text_student, text_teacher, factors)
        grads = 0.5 * (jnp.exp(student - lse_block[0][:, None]) - jnp.exp(teacher - lse_block[1][:, None]) + jnp.exp(student - col_lse[0][None, :]) - jnp.exp(teacher - col_lse[1][None, :]))
        grads = grads.astype(jnp.bfloat16)
        image_grad = jnp.dot(grads, text_student, preferred_element_type=jnp.float32) * factors[0]
        text_grad = text_grad + jnp.dot(grads.T, image_block, preferred_element_type=jnp.float32) * factors[0]
        return (text_grad, image_grad)
    grad_text, image_parts = lax.scan(second_pass, jnp.zeros((BATCH, DS), jnp.float32), (image_blocks, teacher_blocks, row_lse_blocks))
    grad_image = image_parts.reshape(BATCH, DS)
    return (pair_loss, grad_image, grad_text)
```

```python
import functools

import jax
import jax.numpy as jnp
from jax import lax
from jax.experimental import pallas as pl
from jax.experimental.pallas import tpu as pltpu
from jax.sharding import PartitionSpec as P

MESH = pl.DeviceIdType.MESH
F32 = jnp.float32
BF16 = jnp.bfloat16
NT = (((1,), (1,)), ((), ()))


def remote(src, dst, send, recv, device):
    return pltpu.make_async_remote_copy(
        src_ref=src,
        dst_ref=dst,
        send_sem=send,
        recv_sem=recv,
        device_id=device,
        device_id_type=MESH,
    )


def loop(low, high, body):
    def step(i, carry):
        body(i)
        return carry

    lax.fori_loop(low, high, step, 0)


def combine(buf, count, shape):
    row = lax.broadcasted_iota(jnp.int32, shape, 0)
    peak = buf[0]
    for k in range(1, count):
        peak = jnp.maximum(peak, buf[k])
    total = jnp.zeros(shape, F32)
    for k in range(count):
        message = buf[k]
        mean = jnp.broadcast_to(message[3:4], shape)
        total = total + jnp.exp(message - peak) * jnp.where(row == 2, mean, 1.0)
    lse = peak[0:2] + jnp.log(total[0:2])
    loss = lse[0:1] - total[2:3] / total[1:2]
    return lse[0:1], lse[1:2], loss


def kernel(
    zn,
    tn,
    xs_ref,
    xt_ref,
    ts_ref,
    tt_ref,
    ss_ref,
    st_ref,
    loss_ref,
    gi_ref,
    gt_ref,
    buf_s,
    buf_t0,
    buf_t1,
    text_s,
    text_t,
    stu,
    img_s,
    img_t,
    sc_s,
    sc_t,
    e_rs,
    e_rt,
    e_cs,
    e_ct,
    colstat,
    cbuf,
    rbuf,
    colback,
    rowback,
    g_ref,
    gtr_ref,
    q_ref,
    rstage,
    rland,
    istage,
    iland,
    tsend,
    trecv,
    xsend,
    xrecv,
    ssend,
    srecv,
    csend,
    crecv,
    rsend,
    rrecv,
    isend,
    irecv,
    gsend,
    grecv,
):
    pn = 4 * tn
    half = zn // 2
    b = lax.axis_index("batch")
    t = lax.axis_index("tensor")
    z = lax.div(b, 4)
    ylo = lax.rem(lax.div(b, 2), 2)
    core = lax.rem(b, 2)
    yhi = lax.rem(t, 2)
    rb = core * 2 + ylo
    me = rb * tn + t
    rows = xt_ref.shape[0]
    mid = rows // 2
    pairs = ts_ref.shape[0]
    texts = zn * pairs
    images = 4 * rows
    ws = ts_ref.shape[1]
    wt = tt_ref.shape[1]
    wh = wt // 2

    def plane(p):
        r = lax.div(p, tn)
        return (4 * z + lax.rem(r, 2) * 2 + lax.div(r, 2), lax.rem(p, tn))

    def ring(k):
        return (lax.rem(k, zn) * 4 + ylo * 2 + core, t)

    sibling = (b + 1 - 2 * core, t)
    barrier = pltpu.get_barrier_semaphore()

    def greet_plane(d):
        pl.semaphore_signal(
            barrier, inc=1, device_id=plane(lax.rem(me + d, pn)), device_id_type=MESH
        )

    def greet_ring(d):
        pl.semaphore_signal(barrier, inc=1, device_id=ring(z + d), device_id_type=MESH)

    loop(1, zn, greet_ring)
    loop(1, pn, greet_plane)

    bufs = (buf_s, buf_t0, buf_t1)
    buf_s[z] = ts_ref[...]
    buf_t0[z] = tt_ref[:, :wh]
    buf_t1[z] = tt_ref[:, wh:]
    own = xs_ref[...].astype(F32)
    q = ylo * tn + t
    stu[core * 2 * tn + q] = jnp.concatenate([own[:mid], own[mid:]], 1).astype(BF16)

    pl.semaphore_wait(barrier, pn + zn - 2)

    right = ring(z + 1)
    left = ring(z + zn - 1)

    def text_copy(c, way, s):
        if way == 0:
            o = lax.rem(z + zn - s, zn)
        else:
            o = lax.rem(z + s, zn)
        slot = bufs[c].at[o]
        return remote(
            slot, slot, tsend.at[c, way, s], trecv.at[c, way, s], right if way == 0 else left
        )

    def text_wait(c, way, s):
        if way == 0:
            o = lax.rem(z + zn - 1 - s, zn)
        else:
            o = lax.rem(z + 1 + s, zn)
        slot = bufs[c].at[o]
        remote(
            slot, slot, tsend.at[c, way, s], trecv.at[c, way, s], right if way == 0 else left
        ).wait_recv()

    for c in range(3):
        for way in range(2):
            text_copy(c, way, 0).start()

    def block(r, start, size):
        return img_t.at[pl.ds(pl.multiple_of(r * rows + start, mid), size)]

    up = (4 * z + (1 - ylo) * 2 + core, t - yhi + lax.rem(yhi + ylo, 2))
    down = (4 * z + (1 - ylo) * 2 + core, t - yhi + lax.rem(yhi + 1 - ylo, 2))
    other = core * 2 + 1 - ylo
    far = (1 - core) * 2

    def teach(k, src, dst, device):
        return remote(src, dst, xsend.at[k], xrecv.at[k], device)

    to_up = teach(0, xt_ref.at[pl.ds(0, mid)], block(rb, 0, mid), up)
    to_down = teach(1, xt_ref.at[pl.ds(mid, mid)], block(rb, mid, mid), down)
    to_sib = teach(2, xt_ref, block(rb, 0, rows), sibling)
    to_up.start()
    to_down.start()
    to_sib.start()
    img_t[pl.ds(pl.multiple_of(rb * rows, mid), rows)] = xt_ref[...]

    sn = 2 * tn
    own_stu = stu.at[core * sn + q]

    def stu_copy(d):
        p = lax.rem(q + d, sn)
        device = (4 * z + lax.div(p, tn) * 2 + core, lax.rem(p, tn))
        return remote(own_stu, own_stu, ssend.at[d], srecv.at[d], device)

    loop(1, sn, lambda d: stu_copy(d).start())

    def text_step(s):
        for c in range(3):
            for way in range(2):
                text_wait(c, way, s - 1)
                text_copy(c, way, s).start()

    switch = half // 2
    loop(1, switch, text_step)

    def stu_wait(d):
        p = lax.rem(q + sn - d, sn)
        slot = stu.at[core * sn + p]
        remote(slot, slot, ssend.at[d], srecv.at[d], sibling).wait_recv()

    loop(1, sn, stu_wait)
    mine = stu.at[pl.ds(core * sn, sn)]
    stu_sib = remote(mine, mine, ssend.at[0], srecv.at[0], sibling)
    stu_sib.start()
    teach(0, xt_ref.at[pl.ds(0, mid)], block(other, 0, mid), up).wait_recv()
    teach(1, xt_ref.at[pl.ds(mid, mid)], block(other, mid, mid), down).wait_recv()
    to_sib2 = teach(3, block(other, 0, rows), block(other, 0, rows), sibling)
    to_sib2.start()

    loop(switch, half - 1, text_step)

    theirs = stu.at[pl.ds((1 - core) * sn, sn)]
    remote(theirs, theirs, ssend.at[0], srecv.at[0], sibling).wait_recv()
    low = lax.broadcasted_iota(jnp.int32, (mid, 128), 1) < 64

    def unpack(r):
        base = pl.multiple_of(r * rows, mid)
        for x in range(tn // 2):
            one = stu[r * tn + 2 * x].astype(F32)
            two = stu[r * tn + 2 * x + 1].astype(F32)
            cols = pl.ds(x * 128, 128)
            img_s[pl.ds(base, mid), cols] = jnp.where(low, one, pltpu.roll(two, 64, 1)).astype(BF16)
            img_s[pl.ds(pl.multiple_of(base + mid, mid), mid), cols] = jnp.where(
                low, pltpu.roll(one, 64, 1), two
            ).astype(BF16)

    loop(0, 4, unpack)
    far_own = teach(2, xt_ref, block(far + ylo, 0, rows), sibling)
    far_own.wait_recv()
    teach(3, block(other, 0, rows), block(far + 1 - ylo, 0, rows), sibling).wait_recv()

    for c in range(3):
        text_wait(c, 0, half - 2)
        text_copy(c, 0, half - 1).start()
    for c in range(3):
        text_wait(c, 1, half - 2)
    for c in range(3):
        text_wait(c, 0, half - 1)

    def join(i):
        at = pl.ds(pl.multiple_of(i * 2 * pairs, 16), 2 * pairs)
        two = pl.ds(2 * i, 2)
        text_s[at, :] = buf_s[two].astype(F32).reshape(2 * pairs, ws).astype(BF16)
        text_t[at, pl.ds(0, wh)] = buf_t0[two].astype(F32).reshape(2 * pairs, wh).astype(BF16)
        text_t[at, pl.ds(wh, wh)] = buf_t1[two].astype(F32).reshape(2 * pairs, wh).astype(BF16)

    loop(0, zn // 2, join)

    factor_s = ss_ref[0] / jnp.sqrt(jnp.float32(ws))
    factor_t = st_ref[0] / jnp.sqrt(jnp.float32(wt))

    def scores(i):
        at = pl.ds(pl.multiple_of(i * 256, 256), 256)
        sc_s[:, at] = (
            lax.dot_general(text_s[...], img_s[at, :], NT, preferred_element_type=F32) * factor_s
        )
        sc_t[:, at] = (
            lax.dot_general(text_t[...], img_t[at, :], NT, preferred_element_type=F32) * factor_t
        )

    loop(0, images // 256, scores)

    tile = 2 * pairs
    lane = lax.broadcasted_iota(jnp.int32, (tile, 128), 1)

    def fold(x, op):
        out = x[0:8]
        for k in range(1, tile // 8):
            out = op(out, x[8 * k : 8 * k + 8])
        return out

    def first(i, carry):
        at = pl.ds(pl.multiple_of(i * tile, tile), tile)
        s = sc_s[at, :]
        u = sc_t[at, :]
        ps = jnp.max(s, 1, keepdims=True)
        pt = jnp.max(u, 1, keepdims=True)
        es = jnp.exp(s - ps)
        et = jnp.exp(u - pt)
        e_cs[at, :] = es
        e_ct[at, :] = et
        sums = jnp.sum(es, 1, keepdims=True)
        sumt = jnp.sum(et, 1, keepdims=True)
        mean = jnp.sum(et * s, 1, keepdims=True) / sumt
        ls = ps + jnp.log(sums)
        lt = pt + jnp.log(sumt)
        out = jnp.where(lane == 0, ls, lt)
        out = jnp.where(lane == 3, mean, out)
        out = jnp.where(lane == 4, ps, out)
        colstat[at, :] = jnp.where(lane == 5, pt, out)
        return (
            jnp.maximum(carry[0], fold(s, jnp.maximum)),
            jnp.maximum(carry[1], fold(u, jnp.maximum)),
        )

    start = jnp.full((8, images), -jnp.inf, F32)
    peaks = lax.fori_loop(0, zn // 2, first, (start, start))
    cbuf[0] = colstat[...].T[0:4]

    def c_copy(d):
        return remote(cbuf.at[0], cbuf.at[d], csend.at[d], crecv.at[d], ring(z + d))

    loop(1, zn, lambda d: c_copy(d).start())

    row_ps = jnp.max(peaks[0], 0, keepdims=True)
    row_pt = jnp.max(peaks[1], 0, keepdims=True)

    def second(i, carry):
        at = pl.ds(pl.multiple_of(i * tile, tile), tile)
        s = sc_s[at, :]
        es = jnp.exp(s - row_ps)
        et = jnp.exp(sc_t[at, :] - row_pt)
        e_rs[at, :] = es
        e_rt[at, :] = et
        return (
            carry[0] + fold(es, jnp.add),
            carry[1] + fold(et, jnp.add),
            carry[2] + fold(et * s, jnp.add),
        )

    zero = jnp.zeros((8, images), F32)
    row_sums = lax.fori_loop(0, zn // 2, second, (zero, zero, zero))
    rs, rt, rw = [jnp.sum(x, 0, keepdims=True) for x in row_sums]
    shape = (4, images)
    row = lax.broadcasted_iota(jnp.int32, shape, 0)
    rbuf[0] = jnp.where(
        row == 0, row_ps + jnp.log(rs), jnp.where(row == 3, rw / rt, row_pt + jnp.log(rt))
    )

    def r_copy(d):
        device = plane(lax.rem(me + d, pn))
        return remote(rbuf.at[0], rbuf.at[d], rsend.at[d], rrecv.at[d], device)

    loop(1, pn, lambda d: r_copy(d).start())
    loop(1, zn, lambda d: c_copy(d).wait_recv())
    col_s, col_t, col_loss = combine(cbuf, zn, (4, texts))
    row8 = lax.broadcasted_iota(jnp.int32, (8, texts), 0)
    back = jnp.where(row8 == 0, col_s, jnp.where(row8 == 1, col_t, col_loss))
    back = jnp.concatenate([back, jnp.zeros((120, texts), F32)], 0)
    colback[...] = back.T

    loop(1, pn, lambda d: r_copy(d).wait_recv())
    row_s, row_t, row_loss = combine(rbuf, pn, (4, images))
    row_fs = 0.5 * jnp.exp(row_ps - row_s)
    row_ft = 0.5 * jnp.exp(row_pt - row_t)

    def grads(i):
        at = pl.ds(pl.multiple_of(i * tile, tile), tile)
        fs = 0.5 * jnp.exp(colstat[at, 4:5] - colback[at, 0:1])
        ft = 0.5 * jnp.exp(colstat[at, 5:6] - colback[at, 1:2])
        g = e_rs[at, :] * row_fs - e_rt[at, :] * row_ft + e_cs[at, :] * fs - e_ct[at, :] * ft
        g_ref[at, :] = g.astype(BF16)

    loop(0, zn // 2, grads)

    part = jnp.dot(g_ref[...], img_s[...], preferred_element_type=F32)
    q_ref[...] = part.reshape(zn, pairs, ws)
    wg = ws // 2

    def grad_copy(c, way, s):
        return remote(
            rstage.at[c, way, s],
            rland.at[c, way, s],
            gsend.at[c, way, s],
            grecv.at[c, way, s],
            right if way == 0 else left,
        )

    def grad_owner(way, s):
        if way == 0:
            return lax.rem(z + half - s, zn)
        return lax.rem(z + half + 1 + s, zn)

    for c in range(2):
        for way in range(2):
            rstage[c, way, 0] = q_ref[grad_owner(way, 0), :, c * wg : (c + 1) * wg]
            grad_copy(c, way, 0).start()

    def grad_step(s, ways=(0, 1)):
        for c in range(2):
            for way in ways:
                grad_copy(c, way, s - 1).wait_recv()
                rstage[c, way, s] = (
                    q_ref[grad_owner(way, s), :, c * wg : (c + 1) * wg] + rland[c, way, s - 1]
                )
                grad_copy(c, way, s).start()

    gtr_ref[...] = g_ref[...].astype(F32).T.astype(BF16)

    def image_copy(i, e):
        r = lax.rem(rb + i, 4)
        to = lax.rem(t + e, tn)
        k = i * tn + e
        return remote(
            istage.at[i * tn + to],
            iland.at[k],
            isend.at[k],
            irecv.at[k],
            plane(r * tn + to),
        )

    def image_part(i):
        r = lax.rem(rb + i, 4)
        at = pl.ds(pl.multiple_of(r * rows, mid), rows)
        part = jnp.dot(gtr_ref[at, :], text_s[...], preferred_element_type=F32)
        for x in range(tn // 2):
            top = part[:mid, x * 128 : (x + 1) * 128]
            bottom = part[mid:, x * 128 : (x + 1) * 128]
            istage[i * tn + 2 * x] = jnp.where(low, top, pltpu.roll(bottom, 64, 1)).astype(BF16)
            istage[i * tn + 2 * x + 1] = jnp.where(low, pltpu.roll(top, 64, 1), bottom).astype(BF16)

        def send(e):
            @pl.when(i + e > 0)
            def _():
                image_copy(i, e).start()

        loop(0, tn, send)

    def image_and_ring(i):
        image_part(i)
        grad_step(i + 1)

    loop(0, 4, image_and_ring)
    loop(5, half - 1, grad_step)
    grad_step(half - 1, (0,))

    total = istage[t].astype(F32)

    def image_wait(k):
        image_copy(lax.div(k, tn), lax.rem(k, tn)).wait_recv()

    loop(1, pn, image_wait)
    total = lax.fori_loop(1, pn, lambda k, x: x + iland[k].astype(F32), total) * factor_s
    gi_ref[0:mid, :] = total[:, 0:64]
    gi_ref[mid:rows, :] = total[:, 64:128]

    row16 = lax.broadcasted_iota(jnp.int32, (128, images), 0)
    rowback[...] = jnp.where(row16 == 0, row_loss, 0.0).T
    at_row = pl.ds(pl.multiple_of(rb * rows + t * pairs, 8), pairs)
    at_col = pl.ds(pl.multiple_of(z * pairs, 8), pairs)
    loss_ref[...] = 0.5 * (rowback[at_row, 0:1] + colback[at_col, 2:3])

    for c in range(2):
        grad_copy(c, 1, half - 2).wait_recv()
        grad_copy(c, 0, half - 1).wait_recv()
        cols = slice(c * wg, (c + 1) * wg)
        gt_ref[:, cols] = (
            q_ref[z, :, cols] + rland[c, 0, half - 1] + rland[c, 1, half - 2]
        ) * factor_s

    def sent(s):
        for c in range(3):
            for way in range(2):
                text_copy(c, way, s).wait_send()
        for c in range(2):
            for way in range(2):
                grad_copy(c, way, s).wait_send()

    loop(0, half - 1, sent)
    for c in range(3):
        text_copy(c, 0, half - 1).wait_send()
    for c in range(2):
        grad_copy(c, 0, half - 1).wait_send()
    to_up.wait_send()
    to_down.wait_send()
    to_sib.wait_send()
    to_sib2.wait_send()
    stu_sib.wait_send()
    loop(1, sn, lambda d: stu_copy(d).wait_send())
    loop(1, zn, lambda d: c_copy(d).wait_send())

    def sent_plane(d):
        r_copy(d).wait_send()
        image_copy(lax.div(d, tn), lax.rem(d, tn)).wait_send()

    loop(1, pn, sent_plane)


def body(zn, tn, image_student, text_student, image_teacher, text_teacher, ss, st):
    rows = image_teacher.shape[0]
    pairs, ws = text_student.shape
    wt = text_teacher.shape[1]
    texts, images, mid, half = zn * pairs, 4 * rows, rows // 2, zn // 2
    pn, sn = 4 * tn, 2 * tn
    dma = pltpu.SemaphoreType.DMA
    vmem = pl.BlockSpec(memory_space=pltpu.VMEM)
    smem = pl.BlockSpec(memory_space=pltpu.SMEM)
    score = pltpu.VMEM((texts, images), F32)
    loss, grad_image, grad_text = pl.pallas_call(
        functools.partial(kernel, zn, tn),
        out_shape=(
            jax.ShapeDtypeStruct((pairs, 1), F32),
            jax.ShapeDtypeStruct((rows, ws // tn), F32),
            jax.ShapeDtypeStruct((pairs, ws), F32),
        ),
        in_specs=[vmem, vmem, vmem, vmem, smem, smem],
        out_specs=(vmem, vmem, vmem),
        scratch_shapes=[
            pltpu.VMEM((zn, pairs, ws), BF16),
            pltpu.VMEM((zn, pairs, wt // 2), BF16),
            pltpu.VMEM((zn, pairs, wt // 2), BF16),
            pltpu.VMEM((texts, ws), BF16),
            pltpu.VMEM((texts, wt), BF16),
            pltpu.VMEM((pn, mid, 128), BF16),
            pltpu.VMEM((images, ws), BF16),
            pltpu.VMEM((images, wt), BF16),
            score,
            score,
            score,
            score,
            score,
            score,
            pltpu.VMEM((texts, 128), F32),
            pltpu.VMEM((zn, 4, texts), F32),
            pltpu.VMEM((pn, 4, images), F32),
            pltpu.VMEM((texts, 128), F32),
            pltpu.VMEM((images, 128), F32),
            pltpu.VMEM((texts, images), BF16),
            pltpu.VMEM((images, texts), BF16),
            pltpu.VMEM((zn, pairs, ws), F32),
            pltpu.VMEM((2, 2, half, pairs, ws // 2), F32),
            pltpu.VMEM((2, 2, half, pairs, ws // 2), F32),
            pltpu.VMEM((pn, mid, 128), BF16),
            pltpu.VMEM((pn, mid, 128), BF16),
            dma((3, 2, half)),
            dma((3, 2, half)),
            dma((4,)),
            dma((4,)),
            dma((sn,)),
            dma((sn,)),
            dma((zn,)),
            dma((zn,)),
            dma((pn,)),
            dma((pn,)),
            dma((pn,)),
            dma((pn,)),
            dma((2, 2, half)),
            dma((2, 2, half)),
        ],
        compiler_params=pltpu.CompilerParams(
            collective_id=0, has_side_effects=True, vmem_limit_bytes=50 * 2**20
        ),
    )(image_student, image_teacher, text_student, text_teacher, ss, st)
    return loss.reshape(pairs), grad_image, grad_text


def solution(mesh):
    zn = mesh.shape["batch"] // 4
    tn = mesh.shape["tensor"]
    return jax.shard_map(
        functools.partial(body, zn, tn),
        mesh=mesh,
        in_specs=(
            P("batch", "tensor"),
            P(("batch", "tensor"), None),
            P("batch", None),
            P(("batch", "tensor"), None),
            P(),
            P(),
        ),
        out_specs=(P(("batch", "tensor")), P("batch", "tensor"), P(("batch", "tensor"), None)),
        check_vma=False,
    )
```

```python
import functools

import jax
import jax.numpy as jnp
from jax import lax
from jax.experimental import pallas as pl
from jax.experimental.pallas import tpu as pltpu
from jax.sharding import PartitionSpec as P

MESH = pl.DeviceIdType.MESH
F32 = jnp.float32
BF16 = jnp.bfloat16
NN = (((1,), (0,)), ((), ()))
NT = (((1,), (1,)), ((), ()))
SELF = 20


def remote(src, dst, send, recv, device):
    return pltpu.make_async_remote_copy(
        src_ref=src,
        dst_ref=dst,
        send_sem=send,
        recv_sem=recv,
        device_id=device,
        device_id_type=MESH,
    )


def loop(low, high, body):
    def step(i, carry):
        body(i)
        return carry

    lax.fori_loop(low, high, step, 0)


def join_lse(buf, count):
    peak = buf[0]
    for k in range(1, count):
        peak = jnp.maximum(peak, buf[k])
    total = jnp.zeros(peak.shape, F32)
    for k in range(count):
        total = total + jnp.exp(buf[k] - peak)
    return peak + jnp.log(total)


def join_mean(buf, means, lse, count):
    total = jnp.zeros(means[0].shape, F32)
    for k in range(count):
        total = total + jnp.exp(buf[k][1:2] - lse[1:2]) * means[k]
    return total


def kernel(
    zn,
    tn,
    xs_ref,
    xt_ref,
    ts_ref,
    tt_ref,
    ss_ref,
    st_ref,
    loss_ref,
    gi_ref,
    gt_ref,
    xs_v,
    buf_s,
    buf_t0,
    buf_t1,
    text_s,
    text_t,
    text_tr,
    stu,
    img_s,
    img_t,
    sc_s,
    sc_t,
    e_rs,
    e_rt,
    e_cs,
    e_ct,
    colstat,
    cbuf,
    cmean,
    rbuf,
    rmean,
    colback,
    g_ref,
    q_ref,
    p_ref,
    dstage,
    dland,
    hstage,
    hland,
    fstage,
    fland,
    istage,
    iland,
    lsem,
    tsend,
    trecv,
    xsend,
    xrecv,
    ssend,
    srecv,
    csend,
    crecv,
    rsend,
    rrecv,
    isend,
    irecv,
    dsend,
    drecv,
    hsend,
    hrecv,
    fsend,
    frecv,
    cmsend,
    cmrecv,
    rmsend,
    rmrecv,
):
    pn = 4 * tn
    xn = tn // 2
    half = zn // 2
    b = lax.axis_index("batch")
    t = lax.axis_index("tensor")
    z = lax.div(b, 4)
    ylo = lax.rem(lax.div(b, 2), 2)
    core = lax.rem(b, 2)
    x = lax.div(t, 2)
    yhi = lax.rem(t, 2)
    y = yhi * 2 + ylo
    rb = core * 2 + ylo
    rows = xt_ref.shape[0]
    mid = rows // 2
    pairs, ws = ts_ref.shape
    wt = tt_ref.shape[1]
    wh = wt // 2
    wx = ws // tn
    texts = zn * pairs
    images = 4 * rows
    tile = 2 * pairs

    def at_chip(dx, dy, c):
        x2 = lax.rem(x + dx, xn)
        y2 = lax.rem(y + dy, 4)
        return (4 * z + lax.rem(y2, 2) * 2 + c, x2 * 2 + lax.div(y2, 2))

    def ring(d):
        return (lax.rem(z + d, zn) * 4 + ylo * 2 + core, t)

    sibling = (b + 1 - 2 * core, t)
    right = ring(1)
    left = ring(zn - 1)
    near = [right, left, sibling]
    near += [at_chip(d, 0, core) for d in range(1, xn)]
    near += [at_chip(0, d, core) for d in range(1, 4)]
    barrier = pltpu.get_barrier_semaphore()
    for device in near:
        pl.semaphore_signal(barrier, inc=1, device_id=device, device_id_type=MESH)

    bufs = (buf_s, buf_t0, buf_t1)
    own_text = (ts_ref, tt_ref.at[:, pl.ds(0, wh)], tt_ref.at[:, pl.ds(wh, wh)])
    own_xs = pltpu.make_async_copy(xs_ref, xs_v, lsem.at[0])
    own_xs.start()
    local = [pltpu.make_async_copy(own_text[c], bufs[c].at[z], lsem.at[c + 1]) for c in range(3)]

    def block(r, start, size):
        return img_t.at[pl.ds(pl.multiple_of(r * rows + start, mid), size)]

    local.append(pltpu.make_async_copy(xt_ref, block(rb, 0, rows), lsem.at[4]))
    for copy in local:
        copy.start()

    own_xs.wait()
    whole = xs_v[...].astype(F32)
    odd = ylo == 1
    main = jnp.where(odd, whole[:, rows - 128 :], whole[:, :128])
    rest = jnp.where(odd, whole[:, : rows - 128], whole[:, 128:])
    packed = jnp.concatenate([rest[: wx // 2], rest[wx // 2 :]], 1)

    def group(c, y0, y1):
        return ((c * 2 + y0) * 2 + y1) * xn

    own_stu = stu.at[group(core, ylo, yhi) + x]
    own_stu[0:wx, :] = main.astype(BF16)
    own_stu[wx:, :] = packed.astype(BF16)

    pl.semaphore_wait(barrier, len(near))

    def text_copy(c, way, s):
        o = lax.rem(z + (zn - s if way == 0 else s), zn)
        src = own_text[c] if s == 0 else bufs[c].at[o]
        return remote(
            src,
            bufs[c].at[o],
            tsend.at[c, way, s],
            trecv.at[c, way, s],
            right if way == 0 else left,
        )

    def text_wait(c, way, s):
        o = lax.rem(z + (zn - 1 - s if way == 0 else 1 + s), zn)
        slot = bufs[c].at[o]
        remote(
            slot, slot, tsend.at[c, way, s], trecv.at[c, way, s], right if way == 0 else left
        ).wait_recv()

    def text_step(s):
        for c in range(3):
            for way in range(2):
                if s > half - 1 or (way == 1 and s > half - 2):
                    text_wait(c, way, s - 1)
                else:
                    text_wait(c, way, s - 1)
                    text_copy(c, way, s).start()

    for c in range(3):
        for way in range(2):
            text_copy(c, way, 0).start()

    def stu_x(d):
        return remote(own_stu, own_stu, ssend.at[d], srecv.at[d], at_chip(d, 0, core))

    for d in (2, 1, 3):
        stu_x(d).start()

    up = at_chip(0, 1, core)
    down = at_chip(0, 3, core)
    other = core * 2 + 1 - ylo
    far = (1 - core) * 2

    def teach(k, src, dst, device):
        return remote(src, dst, xsend.at[k], xrecv.at[k], device)

    to_up = teach(0, xt_ref.at[pl.ds(0, mid)], block(rb, 0, mid), up)
    to_down = teach(1, xt_ref.at[pl.ds(mid, mid)], block(rb, mid, mid), down)
    to_sib = teach(2, xt_ref, block(rb, 0, rows), sibling)
    to_up.start()
    to_down.start()
    to_sib.start()

    text_step(1)
    for d in range(1, xn):
        slot = stu.at[group(core, ylo, yhi) + lax.rem(x + xn - d, xn)]
        remote(slot, slot, ssend.at[d], srecv.at[d], sibling).wait_recv()

    own_four = stu.at[pl.ds(group(core, ylo, yhi), xn)]

    def stu_y(d):
        return remote(own_four, own_four, ssend.at[3 + d], srecv.at[3 + d], at_chip(0, d, core))

    for d in (2, 1, 3):
        stu_y(d).start()
    text_step(2)
    text_step(3)
    for d in range(1, 4):
        y2 = lax.rem(y + 4 - d, 4)
        slot = stu.at[pl.ds(group(core, lax.rem(y2, 2), lax.div(y2, 2)), xn)]
        remote(slot, slot, ssend.at[3 + d], srecv.at[3 + d], sibling).wait_recv()
    sn = 4 * xn
    mine = stu.at[pl.ds(core * sn, sn)]
    stu_sib = remote(mine, mine, ssend.at[0], srecv.at[0], sibling)
    stu_sib.start()
    teach(0, xt_ref.at[pl.ds(0, mid)], block(other, 0, mid), up).wait_recv()
    teach(1, xt_ref.at[pl.ds(mid, mid)], block(other, mid, mid), down).wait_recv()
    to_sib2 = teach(3, block(other, 0, rows), block(other, 0, rows), sibling)
    to_sib2.start()
    text_step(4)
    for copy in local:
        copy.wait()
    text_step(5)

    theirs = stu.at[pl.ds((1 - core) * sn, sn)]
    remote(theirs, theirs, ssend.at[0], srecv.at[0], sibling).wait_recv()
    low = lax.broadcasted_iota(jnp.int32, (wx // 2, 128), 1) < 64

    def unpack(k):
        c = lax.div(k, tn)
        t2 = lax.rem(k, tn)
        even = stu[group(c, 0, lax.rem(t2, 2)) + lax.div(t2, 2)].astype(F32)
        odds = stu[group(c, 1, lax.rem(t2, 2)) + lax.div(t2, 2)].astype(F32)
        e2 = even[wx:]
        o2 = odds[wx:]
        middle = jnp.concatenate(
            [jnp.where(low, e2, pltpu.roll(o2, 64, 1)), jnp.where(low, pltpu.roll(e2, 64, 1), o2)],
            0,
        )
        at = pl.ds(pl.multiple_of(t2 * wx, wx), wx)
        for k2, part in enumerate((even[:wx], middle, odds[:wx])):
            lanes = pl.ds(pl.multiple_of(c * 2 * rows + k2 * 128, 128), 128)
            img_s[at, lanes] = part.astype(BF16)

    loop(0, 2 * tn, unpack)
    teach(2, xt_ref, block(far + ylo, 0, rows), sibling).wait_recv()
    teach(3, block(other, 0, rows), block(far + 1 - ylo, 0, rows), sibling).wait_recv()

    factor_s = ss_ref[0] / jnp.sqrt(jnp.float32(ws))
    factor_t = st_ref[0] / jnp.sqrt(jnp.float32(wt))
    lane = lax.broadcasted_iota(jnp.int32, (tile, 128), 1)

    def owners(i, last):
        return lax.rem(z + zn - 1 - i, zn), (z if last else lax.rem(z + 1 + i, zn))

    def at_owner(o):
        return pl.ds(pl.multiple_of(o * pairs, 8), pairs)

    def fold(v, op):
        out = v[0:8]
        for k in range(1, tile // 8):
            out = op(out, v[8 * k : 8 * k + 8])
        return out

    def batch(first, end):
        last = end == half

        def at_tile(i):
            return pl.ds(pl.multiple_of(i * tile, tile), tile)

        def join(i):
            o1, o2 = owners(i, last)
            both = lambda buf: jnp.concatenate([buf[o1].astype(F32), buf[o2].astype(F32)], 0)
            text_s[at_tile(i), :] = both(buf_s).astype(BF16)
            text_t[at_tile(i), pl.ds(0, wh)] = both(buf_t0).astype(BF16)
            text_t[at_tile(i), pl.ds(wh, wh)] = both(buf_t1).astype(BF16)

        loop(first, end, join)
        part = pl.ds(first * tile, (end - first) * tile)
        sc_s[part, :] = (
            lax.dot_general(text_s[part, :], img_s[...], NN, preferred_element_type=F32) * factor_s
        )
        sc_t[part, :] = (
            lax.dot_general(text_t[part, :], img_t[...], NT, preferred_element_type=F32) * factor_t
        )

        def columns(i, carry):
            at = at_tile(i)
            s = sc_s[at, :]
            u = sc_t[at, :]
            ps = jnp.max(s, 1, keepdims=True)
            pt = jnp.max(u, 1, keepdims=True)
            es = jnp.exp(s - ps)
            et = jnp.exp(u - pt)
            e_cs[at, :] = es
            e_ct[at, :] = et
            sums = jnp.sum(es, 1, keepdims=True)
            sumt = jnp.sum(et, 1, keepdims=True)
            mean = jnp.sum(et * s, 1, keepdims=True) / sumt
            out = jnp.where(lane == 0, ps + jnp.log(sums), pt + jnp.log(sumt))
            out = jnp.where(lane == 2, mean, out)
            out = jnp.where(lane == 4, ps, out)
            out = jnp.where(lane == 5, pt, out)
            o1, o2 = owners(i, last)
            colstat[at_owner(o1), :] = out[:pairs]
            colstat[at_owner(o2), :] = out[pairs:]
            return (
                jnp.maximum(carry[0], fold(s, jnp.maximum)),
                jnp.maximum(carry[1], fold(u, jnp.maximum)),
            )

        none = jnp.full((8, images), -jnp.inf, F32)
        peaks = lax.fori_loop(first, end, columns, (none, none))
        row_ps = jnp.max(peaks[0], 0, keepdims=True)
        row_pt = jnp.max(peaks[1], 0, keepdims=True)

        def by_rows(i, carry):
            at = at_tile(i)
            s = sc_s[at, :]
            es = jnp.exp(s - row_ps)
            et = jnp.exp(sc_t[at, :] - row_pt)
            e_rs[at, :] = es
            e_rt[at, :] = et
            return (
                carry[0] + fold(es, jnp.add),
                carry[1] + fold(et, jnp.add),
                carry[2] + fold(et * s, jnp.add),
            )

        zero = jnp.zeros((8, images), F32)
        sums = lax.fori_loop(first, end, by_rows, (zero, zero, zero))
        return [row_ps, row_pt] + [jnp.sum(v, 0, keepdims=True) for v in sums]

    cuts = [0, 3, 5, 7, 8]
    stats = [batch(0, 3)]
    text_step(6)
    stats.append(batch(3, 5))
    text_step(7)
    stats.append(batch(5, 7))
    for c in range(3):
        text_wait(c, 0, half - 1)
    stats.append(batch(7, 8))

    across = colstat[...].T
    cbuf[zn - 1] = across[0:2]
    cmean[zn - 1] = across[2:3]

    def ring_place(j):
        return half + (1 - 2 * lax.rem(j, 2)) * lax.div(j + 1, 2)

    def c_copy(j):
        return remote(
            cbuf.at[zn - 1], cbuf.at[j], csend.at[j], crecv.at[j], ring(ring_place(j))
        )

    def cm_copy(j):
        return remote(
            cmean.at[zn - 1], cmean.at[j], cmsend.at[j], cmrecv.at[j], ring(ring_place(j))
        )

    loop(0, zn - 1, lambda j: c_copy(j).start())

    def merged(peak, total):
        top = functools.reduce(jnp.maximum, [s[peak] for s in stats])
        scaled = [jnp.exp(s[peak] - top) for s in stats]
        return top, scaled, sum(f * s[total] for f, s in zip(scaled, stats))

    top_s, _, rs = merged(0, 2)
    top_t, scaled, rt = merged(1, 3)
    rw = sum(f * s[4] for f, s in zip(scaled, stats))
    row = lax.broadcasted_iota(jnp.int32, (2, images), 0)
    rbuf[SELF] = jnp.where(row == 0, top_s + jnp.log(rs), top_t + jnp.log(rt))
    rmean[SELF] = rw / rt

    def chip_of(e):
        return lax.rem(e + 2, 4), lax.rem(lax.div(e, 4) + 2, 4)

    def to_plane(f):
        def each(e):
            for dc in range(2):
                if dc == 0:

                    @pl.when(e != SELF // 2)
                    def _():
                        f(e, dc)

                else:
                    f(e, dc)

        loop(0, 4 * xn, each)

    def plane_copy(buf, send, recv):
        def make(e, dc):
            dx, dy = chip_of(e)
            k = 2 * e + dc
            device = at_chip(dx, dy, 1 - core if dc else core)
            return remote(buf.at[SELF], buf.at[k], send.at[k], recv.at[k], device)

        return make

    r_copy = plane_copy(rbuf, rsend, rrecv)
    rm_copy = plane_copy(rmean, rmsend, rmrecv)
    to_plane(lambda e, dc: r_copy(e, dc).start())
    text_tr[...] = text_s[...].astype(F32).T.astype(BF16)

    loop(0, zn - 1, lambda j: c_copy(j).wait_recv())
    col_lse = join_lse(cbuf, zn)
    colback[...] = jnp.concatenate([col_lse, jnp.zeros((126, texts), F32)], 0).T
    to_plane(lambda e, dc: r_copy(e, dc).wait_recv())
    row_lse = join_lse(rbuf, pn)

    for k in range(4):
        row_fs = 0.5 * jnp.exp(stats[k][0] - row_lse[0:1])
        row_ft = 0.5 * jnp.exp(stats[k][1] - row_lse[1:2])

        def grads(i, last=k == 3, row_fs=row_fs, row_ft=row_ft):
            at = pl.ds(pl.multiple_of(i * tile, tile), tile)
            o1, o2 = owners(i, last)
            here = jnp.concatenate([colstat[at_owner(o1), :], colstat[at_owner(o2), :]], 0)
            lse = jnp.concatenate([colback[at_owner(o1), :], colback[at_owner(o2), :]], 0)
            fs = 0.5 * jnp.exp(here[:, 4:5] - lse[:, 0:1])
            ft = 0.5 * jnp.exp(here[:, 5:6] - lse[:, 1:2])
            g = e_rs[at, :] * row_fs - e_rt[at, :] * row_ft + e_cs[at, :] * fs - e_ct[at, :] * ft
            g_ref[at, :] = g.astype(BF16)

        loop(cuts[k], cuts[k + 1], grads)

    part = lax.dot_general(g_ref[...], img_s[...], NT, preferred_element_type=F32)
    q_ref[...] = part.reshape(zn, pairs, ws)

    def place(way, d):
        return 2 * (half - 1) if d == half else 2 * (d - 1) + (1 if way == 0 else 0)

    def hop(way, d):
        return ring(d if way == 0 else zn - d)

    quarter = half // 2
    relays = [(0, quarter)] + [(w, d) for d in range(quarter - 1, 0, -1) for w in range(2)]
    directs = [(w, d) for d in range(quarter - 1, 0, -1) for w in range(2)]

    def h_copy(k):
        return remote(hstage.at[k], hland.at[k], hsend.at[k], hrecv.at[k], hop(*relays[k]))

    def d_copy(k):
        return remote(dstage.at[k], dland.at[k], dsend.at[k], drecv.at[k], hop(*directs[k]))

    def f_copy(way):
        return remote(
            fstage.at[way], fland.at[way], fsend.at[way], frecv.at[way], hop(way, quarter)
        )

    for k, (way, d) in enumerate(relays):
        hstage[k] = q_ref[place(way, d + quarter)].astype(BF16)
        h_copy(k).start()
    for k, (way, d) in enumerate(directs):
        dstage[k] = q_ref[place(way, d)].astype(BF16)
        d_copy(k).start()

    p_ref[...] = jnp.dot(text_tr[...], g_ref[...], preferred_element_type=F32)

    def pack(k):
        c = lax.div(k, tn)
        t2 = lax.rem(k, tn)
        at = pl.ds(pl.multiple_of(t2 * wx, wx), wx)

        def third(j):
            return p_ref[at, pl.ds(pl.multiple_of(c * 2 * rows + j * 128, 128), 128)]

        middle = third(1)
        m1 = middle[: wx // 2]
        m2 = middle[wx // 2 :]
        even = group(c, 0, lax.rem(t2, 2)) + lax.div(t2, 2)
        odds = group(c, 1, lax.rem(t2, 2)) + lax.div(t2, 2)
        istage[even, pl.ds(0, wx), :] = third(0).astype(BF16)
        istage[odds, pl.ds(0, wx), :] = third(2).astype(BF16)
        istage[even, pl.ds(wx, wx // 2), :] = jnp.where(low, m1, pltpu.roll(m2, 64, 1)).astype(BF16)
        istage[odds, pl.ds(wx, wx // 2), :] = jnp.where(low, pltpu.roll(m1, 64, 1), m2).astype(BF16)

    loop(0, 2 * tn, pack)

    def i_copy(e, dc):
        dx, dy = chip_of(e)
        c = 1 - core if dc else core
        y2 = lax.rem(y + dy, 4)
        src = istage.at[group(c, lax.rem(y2, 2), lax.div(y2, 2)) + lax.rem(x + dx, xn)]
        k = 2 * e + dc
        return remote(src, iland.at[k], isend.at[k], irecv.at[k], at_chip(dx, dy, c))

    to_plane(lambda e, dc: i_copy(e, dc).start())

    for k in range(len(relays)):
        h_copy(k).wait_recv()
    for way in range(2):
        total = q_ref[place(way, quarter)]
        for k, (w, d) in enumerate(relays):
            if w == way:
                total = total + hland[k].astype(F32)
        fstage[way] = total.astype(BF16)
        f_copy(way).start()

    loop(0, zn - 1, lambda j: cm_copy(j).start())
    to_plane(lambda e, dc: rm_copy(e, dc).start())

    to_plane(lambda e, dc: i_copy(e, dc).wait_recv())
    total = istage[group(core, ylo, yhi) + x].astype(F32)
    for k in range(pn):
        if k != SELF:
            total = total + iland[k].astype(F32)
    total = total * factor_s
    main = total[:wx]
    rest = jnp.concatenate([total[wx:, :64], total[wx:, 64:]], 0)
    gi_ref[...] = jnp.where(
        odd, jnp.concatenate([rest, main], 1), jnp.concatenate([main, rest], 1)
    )

    total = q_ref[zn - 1]
    for k in range(len(directs)):
        d_copy(k).wait_recv()
        total = total + dland[k].astype(F32)
    for way in range(2):
        f_copy(way).wait_recv()
        total = total + fland[way].astype(F32)
    gt_ref[...] = total * factor_s

    loop(0, zn - 1, lambda j: cm_copy(j).wait_recv())
    to_plane(lambda e, dc: rm_copy(e, dc).wait_recv())
    col_loss = col_lse[0:1] - join_mean(cbuf, cmean, col_lse, zn)
    row_loss = row_lse[0:1] - join_mean(rbuf, rmean, row_lse, pn)
    own_col = pltpu.roll(jnp.broadcast_to(col_loss, (8, texts)), texts - z * pairs, 1)
    own_row = pltpu.roll(
        jnp.broadcast_to(row_loss, (8, images)), images - rb * rows - t * pairs, 1
    )
    loss_ref[...] = 0.5 * (own_col[0:1, 0:pairs] + own_row[0:1, 0:pairs])

    for s in range(half):
        for c in range(3):
            for way in range(2):
                if way == 0 or s < half - 1:
                    text_copy(c, way, s).wait_send()
    for d in range(1, xn):
        stu_x(d).wait_send()
    for d in range(1, 4):
        stu_y(d).wait_send()
    for copy in (to_up, to_down, to_sib, to_sib2, stu_sib):
        copy.wait_send()
    for k in range(len(relays)):
        h_copy(k).wait_send()
    for k in range(len(directs)):
        d_copy(k).wait_send()
    for way in range(2):
        f_copy(way).wait_send()

    def sent(j):
        c_copy(j).wait_send()
        cm_copy(j).wait_send()

    loop(0, zn - 1, sent)

    def sent_plane(e, dc):
        r_copy(e, dc).wait_send()
        rm_copy(e, dc).wait_send()
        i_copy(e, dc).wait_send()

    to_plane(sent_plane)


def body(zn, tn, image_student, text_student, image_teacher, text_teacher, ss, st):
    rows = image_teacher.shape[0]
    pairs, ws = text_student.shape
    wt = text_teacher.shape[1]
    wx = ws // tn
    texts, images, half = zn * pairs, 4 * rows, zn // 2
    pn = 4 * tn
    high = wx * rows // 128
    dma = pltpu.SemaphoreType.DMA
    anywhere = pl.BlockSpec(memory_space=pl.ANY)
    vmem = pl.BlockSpec(memory_space=pltpu.VMEM)
    smem = pl.BlockSpec(memory_space=pltpu.SMEM)
    score = pltpu.VMEM((texts, images), F32)
    loss, grad_image, grad_text = pl.pallas_call(
        functools.partial(kernel, zn, tn),
        out_shape=(
            jax.ShapeDtypeStruct((1, pairs), F32),
            jax.ShapeDtypeStruct((wx, rows), F32),
            jax.ShapeDtypeStruct((pairs, ws), F32),
        ),
        in_specs=[anywhere] * 4 + [smem, smem],
        out_specs=(vmem, vmem, vmem),
        scratch_shapes=[
            pltpu.VMEM((wx, rows), BF16),
            pltpu.VMEM((zn, pairs, ws), BF16),
            pltpu.VMEM((zn, pairs, wt // 2), BF16),
            pltpu.VMEM((zn, pairs, wt // 2), BF16),
            pltpu.VMEM((texts, ws), BF16),
            pltpu.VMEM((texts, wt), BF16),
            pltpu.VMEM((ws, texts), BF16),
            pltpu.VMEM((pn, high, 128), BF16),
            pltpu.VMEM((ws, images), BF16),
            pltpu.VMEM((images, wt), BF16),
            score,
            score,
            score,
            score,
            score,
            score,
            pltpu.VMEM((texts, 128), F32),
            pltpu.VMEM((zn, 2, texts), F32),
            pltpu.VMEM((zn, 1, texts), F32),
            pltpu.VMEM((pn, 2, images), F32),
            pltpu.VMEM((pn, 1, images), F32),
            pltpu.VMEM((texts, 128), F32),
            pltpu.VMEM((texts, images), BF16),
            pltpu.VMEM((zn, pairs, ws), F32),
            pltpu.VMEM((ws, images), F32),
            pltpu.VMEM((half - 2, pairs, ws), BF16),
            pltpu.VMEM((half - 2, pairs, ws), BF16),
            pltpu.VMEM((half - 1, pairs, ws), BF16),
            pltpu.VMEM((half - 1, pairs, ws), BF16),
            pltpu.VMEM((2, pairs, ws), BF16),
            pltpu.VMEM((2, pairs, ws), BF16),
            pltpu.VMEM((pn, high, 128), BF16),
            pltpu.VMEM((pn, high, 128), BF16),
            dma((5,)),
            dma((3, 2, half)),
            dma((3, 2, half)),
            dma((4,)),
            dma((4,)),
            dma((8,)),
            dma((8,)),
            dma((zn,)),
            dma((zn,)),
            dma((pn,)),
            dma((pn,)),
            dma((pn,)),
            dma((pn,)),
            dma((half - 2,)),
            dma((half - 2,)),
            dma((half - 1,)),
            dma((half - 1,)),
            dma((2,)),
            dma((2,)),
            dma((zn,)),
            dma((zn,)),
            dma((pn,)),
            dma((pn,)),
        ],
        compiler_params=pltpu.CompilerParams(
            collective_id=0, has_side_effects=True, vmem_limit_bytes=62 * 2**20
        ),
    )(image_student.T, image_teacher, text_student, text_teacher, ss, st)
    return loss.reshape(pairs), grad_image.T, grad_text


def solution(mesh):
    zn = mesh.shape["batch"] // 4
    tn = mesh.shape["tensor"]
    return jax.shard_map(
        functools.partial(body, zn, tn),
        mesh=mesh,
        in_specs=(
            P("batch", "tensor"),
            P(("batch", "tensor"), None),
            P("batch", None),
            P(("batch", "tensor"), None),
            P(),
            P(),
        ),
        out_specs=(P(("batch", "tensor")), P("batch", "tensor"), P(("batch", "tensor"), None)),
        check_vma=False,
    )
```

```python
import functools

import jax
import jax.numpy as jnp
from jax import lax
from jax.experimental import pallas as pl
from jax.experimental.pallas import tpu as pltpu
from jax.sharding import PartitionSpec as P

MESH = pl.DeviceIdType.MESH
F32 = jnp.float32
BF16 = jnp.bfloat16
NN = (((1,), (0,)), ((), ()))
NT = (((1,), (1,)), ((), ()))


def remote(src, dst, send, recv, device):
    return pltpu.make_async_remote_copy(
        src_ref=src,
        dst_ref=dst,
        send_sem=send,
        recv_sem=recv,
        device_id=device,
        device_id_type=MESH,
    )


def loop(low, high, body):
    def step(i, carry):
        body(i)
        return carry

    lax.fori_loop(low, high, step, 0)


def join_lse(parts):
    peak = functools.reduce(jnp.maximum, parts)
    return peak + jnp.log(sum(jnp.exp(v - peak) for v in parts))


def join_mean(lses, means, lse):
    return sum(jnp.exp(v - lse) * m for v, m in zip(lses, means))


def kernel(
    zn,
    tn,
    xs_ref,
    xt_ref,
    ts_ref,
    tt_ref,
    ss_ref,
    st_ref,
    loss_ref,
    gi_ref,
    gt_ref,
    xs_v,
    buf_a,
    buf_b,
    text_s,
    text_t,
    text_tr,
    stu,
    img_s,
    img_t,
    sc_s,
    sc_t,
    e_rs,
    e_rt,
    e_cs,
    e_ct,
    colstat,
    cbuf,
    cmean,
    rbuf,
    colback,
    g_ref,
    q_ref,
    p_ref,
    dstage,
    dland,
    hstage,
    hland,
    fstage,
    fland,
    sstage,
    sland,
    istage,
    iland,
    rsib,
    lsem,
    tsend,
    trecv,
    xsend,
    xrecv,
    ssend,
    srecv,
    send,
    recv,
):
    xn = tn // 2
    half = zn // 2
    b = lax.axis_index("batch")
    t = lax.axis_index("tensor")
    z = lax.div(b, 4)
    ylo = lax.rem(lax.div(b, 2), 2)
    core = lax.rem(b, 2)
    x = lax.div(t, 2)
    yhi = lax.rem(t, 2)
    y = yhi * 2 + ylo
    rb = core * 2 + ylo
    rows = xt_ref.shape[0]
    mid = rows // 2
    pairs, ws = ts_ref.shape
    wt = tt_ref.shape[1]
    wc = (ws + wt) // 2
    wa = wc - ws
    wx = ws // tn
    texts = zn * pairs
    images = 4 * rows
    tile = 2 * pairs

    def at_chip(dx, dy, c):
        x2 = lax.rem(x + dx, xn)
        y2 = lax.rem(y + dy, 4)
        return (4 * z + lax.rem(y2, 2) * 2 + c, x2 * 2 + lax.div(y2, 2))

    def ring(d):
        return (lax.rem(z + d, zn) * 4 + ylo * 2 + core, t)

    sibling = (b + 1 - 2 * core, t)
    right = ring(1)
    left = ring(zn - 1)
    near = [right, left, sibling]
    near += [at_chip(d, 0, core) for d in range(1, xn)]
    near += [at_chip(0, d, core) for d in range(1, 4)]
    barrier = pltpu.get_barrier_semaphore()
    for device in near:
        pl.semaphore_signal(barrier, inc=1, device_id=device, device_id_type=MESH)

    bufs = (buf_a, buf_b)
    texts_in = [
        pltpu.make_async_copy(ts_ref, buf_a.at[z, :, pl.ds(0, ws)], lsem.at[1]),
        pltpu.make_async_copy(
            tt_ref.at[:, pl.ds(0, wa)], buf_a.at[z, :, pl.ds(ws, wa)], lsem.at[2]
        ),
        pltpu.make_async_copy(tt_ref.at[:, pl.ds(wa, wc)], buf_b.at[z], lsem.at[3]),
    ]
    for copy in texts_in:
        copy.start()
    own_xs = pltpu.make_async_copy(xs_ref, xs_v, lsem.at[0])
    own_xs.start()

    def block(r, start, size):
        return img_t.at[pl.ds(pl.multiple_of(r * rows + start, mid), size)]

    own_xt = pltpu.make_async_copy(xt_ref, block(rb, 0, rows), lsem.at[4])
    own_xt.start()

    for copy in texts_in:
        copy.wait()
    pl.semaphore_wait(barrier, len(near))

    def text_copy(c, way, s):
        o = lax.rem(z + (zn - s if way == 0 else s), zn)
        slot = bufs[c].at[o]
        return remote(
            slot, slot, tsend.at[c], trecv.at[c, way, s], right if way == 0 else left
        )

    def text_wait(c, way, s):
        o = lax.rem(z + (zn - 1 - s if way == 0 else 1 + s), zn)
        slot = bufs[c].at[o]
        remote(slot, slot, tsend.at[c], trecv.at[c, way, s], right).wait_recv()

    def text_step(s):
        for c in range(2):
            for way in range(2):
                if s > half - 1 or (way == 1 and s > half - 2):
                    text_wait(c, way, s - 1)
                else:
                    text_wait(c, way, s - 1)
                    text_copy(c, way, s).start()

    for c in range(2):
        for way in range(2):
            text_copy(c, way, 0).start()

    up = at_chip(0, 1, core)
    down = at_chip(0, 3, core)
    other = core * 2 + 1 - ylo
    far = (1 - core) * 2

    def teach(k, src, dst, device):
        return remote(src, dst, xsend.at[k], xrecv.at[k], device)

    to_up = teach(0, xt_ref.at[pl.ds(0, mid)], block(rb, 0, mid), up)
    to_down = teach(0, xt_ref.at[pl.ds(mid, mid)], block(rb, mid, mid), down)
    to_sib = teach(1, xt_ref, block(rb, 0, rows), sibling)
    to_up.start()
    to_down.start()
    to_sib.start()

    own_xs.wait()
    whole = xs_v[...].astype(F32)
    odd = ylo == 1
    main = jnp.where(odd, whole[:, rows - 128 :], whole[:, :128])
    rest = jnp.where(odd, whole[:, : rows - 128], whole[:, 128:])
    packed = jnp.concatenate([rest[: wx // 2], rest[wx // 2 :]], 1)

    def stu_place(c, x2, y0, y1):
        return (c * xn + x2) * 4 + y0 * 2 + y1

    own_stu = stu.at[stu_place(core, x, ylo, yhi)]
    own_stu[0:wx, :] = main.astype(BF16)
    own_stu[wx:, :] = packed.astype(BF16)

    def stu_y(d):
        return remote(own_stu, own_stu, ssend.at[0], srecv.at[0], at_chip(0, d, core))

    for d in (2, 1, 3):
        stu_y(d).start()

    text_step(1)
    def stu_wait(k, count):
        some = stu.at[pl.ds(0, count)]
        remote(some, some, ssend.at[k], srecv.at[k], sibling).wait_recv()

    stu_wait(0, 3)
    own_four = stu.at[pl.ds(stu_place(core, x, 0, 0), 4)]

    def stu_x(d):
        return remote(own_four, own_four, ssend.at[1], srecv.at[1], at_chip(d, 0, core))

    for d in (2, 1, 3):
        stu_x(d).start()
    text_step(2)
    text_step(3)
    sn = 4 * xn
    stu_wait(1, sn - 4)
    mine = stu.at[pl.ds(core * sn, sn)]
    stu_sib = remote(mine, mine, ssend.at[2], srecv.at[2], sibling)
    stu_sib.start()
    teach(0, xt_ref, block(other, 0, rows), up).wait_recv()
    to_sib2 = teach(1, block(other, 0, rows), block(other, 0, rows), sibling)
    to_sib2.start()
    text_step(4)
    own_xt.wait()
    text_step(5)

    stu_wait(2, sn)
    low = lax.broadcasted_iota(jnp.int32, (wx // 2, 128), 1) < 64

    def unpack(k):
        c = lax.div(k, tn)
        t2 = lax.rem(k, tn)
        even = stu[stu_place(c, lax.div(t2, 2), 0, lax.rem(t2, 2))].astype(F32)
        odds = stu[stu_place(c, lax.div(t2, 2), 1, lax.rem(t2, 2))].astype(F32)
        e2 = even[wx:]
        o2 = odds[wx:]
        middle = jnp.concatenate(
            [jnp.where(low, e2, pltpu.roll(o2, 64, 1)), jnp.where(low, pltpu.roll(e2, 64, 1), o2)],
            0,
        )
        at = pl.ds(pl.multiple_of(t2 * wx, wx), wx)
        for k2, part in enumerate((even[:wx], middle, odds[:wx])):
            lanes = pl.ds(pl.multiple_of(c * 2 * rows + k2 * 128, 128), 128)
            img_s[at, lanes] = part.astype(BF16)

    loop(0, 2 * tn, unpack)
    both_far = img_t.at[pl.ds(pl.multiple_of(far * rows, mid), 2 * rows)]
    teach(1, both_far, both_far, sibling).wait_recv()

    factor_s = ss_ref[0] / jnp.sqrt(jnp.float32(ws))
    factor_t = st_ref[0] / jnp.sqrt(jnp.float32(wt))
    lane = lax.broadcasted_iota(jnp.int32, (tile, 128), 1)

    def owners(i, last):
        return lax.rem(z + zn - 1 - i, zn), (z if last else lax.rem(z + 1 + i, zn))

    def at_owner(o):
        return pl.ds(pl.multiple_of(o * pairs, 8), pairs)

    def fold(v, op):
        out = v[0:8]
        for k in range(1, tile // 8):
            out = op(out, v[8 * k : 8 * k + 8])
        return out

    def batch(first, end):
        last = end == half

        def at_tile(i):
            return pl.ds(pl.multiple_of(i * tile, tile), tile)

        def join(i):
            o1, o2 = owners(i, last)
            both = lambda buf: jnp.concatenate([buf[o1].astype(F32), buf[o2].astype(F32)], 0)
            one = both(buf_a).astype(BF16)
            text_s[at_tile(i), :] = one[:, :ws]
            text_t[at_tile(i), pl.ds(0, wa)] = one[:, ws:]
            text_t[at_tile(i), pl.ds(wa, wc)] = both(buf_b).astype(BF16)

        loop(first, end, join)
        part = pl.ds(first * tile, (end - first) * tile)
        sc_s[part, :] = (
            lax.dot_general(text_s[part, :], img_s[...], NN, preferred_element_type=F32) * factor_s
        )
        sc_t[part, :] = (
            lax.dot_general(text_t[part, :], img_t[...], NT, preferred_element_type=F32) * factor_t
        )

        def columns(i, carry):
            at = at_tile(i)
            s = sc_s[at, :]
            u = sc_t[at, :]
            ps = jnp.max(s, 1, keepdims=True)
            pt = jnp.max(u, 1, keepdims=True)
            es = jnp.exp(s - ps)
            et = jnp.exp(u - pt)
            e_cs[at, :] = es
            e_ct[at, :] = et
            sums = jnp.sum(es, 1, keepdims=True)
            sumt = jnp.sum(et, 1, keepdims=True)
            mean = jnp.sum(et * s, 1, keepdims=True) / sumt
            out = jnp.where(lane == 0, ps + jnp.log(sums), pt + jnp.log(sumt))
            out = jnp.where(lane == 2, mean, out)
            out = jnp.where(lane == 4, ps, out)
            out = jnp.where(lane == 5, pt, out)
            o1, o2 = owners(i, last)
            colstat[at_owner(o1), :] = out[:pairs]
            colstat[at_owner(o2), :] = out[pairs:]
            return (
                jnp.maximum(carry[0], fold(s, jnp.maximum)),
                jnp.maximum(carry[1], fold(u, jnp.maximum)),
            )

        none = jnp.full((8, images), -jnp.inf, F32)
        peaks = lax.fori_loop(first, end, columns, (none, none))
        row_ps = jnp.max(peaks[0], 0, keepdims=True)
        row_pt = jnp.max(peaks[1], 0, keepdims=True)

        def by_rows(i, carry):
            at = at_tile(i)
            s = sc_s[at, :]
            es = jnp.exp(s - row_ps)
            et = jnp.exp(sc_t[at, :] - row_pt)
            e_rs[at, :] = es
            e_rt[at, :] = et
            return (
                carry[0] + fold(es, jnp.add),
                carry[1] + fold(et, jnp.add),
                carry[2] + fold(et * s, jnp.add),
            )

        zero = jnp.zeros((8, images), F32)
        sums = lax.fori_loop(first, end, by_rows, (zero, zero, zero))
        return [row_ps, row_pt] + [jnp.sum(v, 0, keepdims=True) for v in sums]

    cuts = [0, 2, 4, 7, 8]
    stats = [batch(0, 2)]
    text_step(6)
    stats.append(batch(2, 4))
    text_step(7)
    stats.append(batch(4, 7))
    for c in range(2):
        text_wait(c, 0, half - 1)
    stats.append(batch(7, 8))

    across = colstat[...].T
    cbuf[zn - 1] = across[0:2]
    cmean[zn - 1] = across[2:3]

    def ring_place(j):
        return half + (1 - 2 * lax.rem(j, 2)) * lax.div(j + 1, 2)

    def c_copy(j):
        return remote(cbuf.at[zn - 1], cbuf.at[j], send.at[0], recv.at[0], ring(ring_place(j)))

    def cm_copy(j):
        return remote(cmean.at[zn - 1], cmean.at[j], send.at[1], recv.at[1], ring(ring_place(j)))

    def whole_of(buf, k, count):
        some = buf.at[pl.ds(0, count)]
        return remote(some, some, send.at[k], recv.at[k], sibling)

    loop(0, zn - 1, lambda j: c_copy(j).start())

    def merged(peak, total):
        top = functools.reduce(jnp.maximum, [s[peak] for s in stats])
        scaled = [jnp.exp(s[peak] - top) for s in stats]
        return top, scaled, sum(f * s[total] for f, s in zip(scaled, stats))

    top_s, _, rs = merged(0, 2)
    top_t, scaled, rt = merged(1, 3)
    rw = sum(f * s[4] for f, s in zip(scaled, stats))
    row = lax.broadcasted_iota(jnp.int32, (4, images), 0)

    def rows_of(ls, lt, mean):
        return jnp.where(row == 0, ls, jnp.where(row == 1, lt, mean))

    rsib[0] = rows_of(top_s + jnp.log(rs), top_t + jnp.log(rt), rw / rt)
    r_sib = remote(rsib.at[0], rsib.at[1], send.at[2], recv.at[2], sibling)
    r_sib.start()
    r_sib.wait_recv()
    chip = [join_lse([rsib[0][k : k + 1], rsib[1][k : k + 1]]) for k in range(2)]
    chip_mean = join_mean(
        [rsib[0][1:2], rsib[1][1:2]], [rsib[0][2:3], rsib[1][2:3]], chip[1]
    )
    rbuf[sn - 1] = rows_of(chip[0], chip[1], chip_mean)

    def chip_at(m):
        e = m + lax.div(m, 10)
        return lax.rem(e + 2, 4), lax.rem(lax.div(e, 4) + 2, 4)

    def r_copy(m):
        dx, dy = chip_at(m)
        return remote(rbuf.at[sn - 1], rbuf.at[m], send.at[3], recv.at[3], at_chip(dx, dy, core))

    loop(0, sn - 1, lambda m: r_copy(m).start())
    loop(0, zn - 1, lambda j: cm_copy(j).start())
    text_tr[...] = text_s[...].astype(F32).T.astype(BF16)

    whole_of(cbuf, 0, zn - 1).wait_recv()
    col_lse = join_lse([cbuf[k] for k in range(zn)])
    colback[...] = jnp.concatenate([col_lse, jnp.zeros((126, texts), F32)], 0).T
    whole_of(rbuf, 3, sn - 1).wait_recv()
    row_lse = join_lse([rbuf[k] for k in range(sn)])

    def grad_tiles(k):
        row_fs = 0.5 * jnp.exp(stats[k][0] - row_lse[0:1])
        row_ft = 0.5 * jnp.exp(stats[k][1] - row_lse[1:2])

        def grads(i, last=k == 3, row_fs=row_fs, row_ft=row_ft):
            at = pl.ds(pl.multiple_of(i * tile, tile), tile)
            o1, o2 = owners(i, last)
            here = jnp.concatenate([colstat[at_owner(o1), :], colstat[at_owner(o2), :]], 0)
            lse = jnp.concatenate([colback[at_owner(o1), :], colback[at_owner(o2), :]], 0)
            fs = 0.5 * jnp.exp(here[:, 4:5] - lse[:, 0:1])
            ft = 0.5 * jnp.exp(here[:, 5:6] - lse[:, 1:2])
            g = e_rs[at, :] * row_fs - e_rt[at, :] * row_ft + e_cs[at, :] * fs - e_ct[at, :] * ft
            g_ref[at, :] = g.astype(BF16)

        loop(cuts[k], cuts[k + 1], grads)

    def text_part(first, end):
        at = pl.ds(first * tile, (end - first) * tile)
        part = lax.dot_general(g_ref[at, :], img_s[...], NT, preferred_element_type=F32)
        q_ref[2 * first : 2 * end] = part.reshape(2 * (end - first), pairs, ws)


    def place(way, d):
        return 2 * (half - 1) if d == half else 2 * (d - 1) + (1 if way == 0 else 0)

    def hop(way, d):
        return ring(d if way == 0 else zn - d)

    quarter = half // 2
    relays = [(0, quarter)] + [(w, d) for d in range(quarter - 1, 0, -1) for w in range(2)]
    directs = [(w, d) for d in range(quarter - 1, 0, -1) for w in range(2)]

    def h_copy(k):
        return remote(hstage.at[k], hland.at[k], send.at[4], recv.at[4], hop(*relays[k]))

    def d_copy(k):
        return remote(dstage.at[k], dland.at[k], send.at[5], recv.at[5], hop(*directs[k]))

    def f_copy(way):
        return remote(
            fstage.at[way], fland.at[way], send.at[6], recv.at[6], hop(way, quarter)
        )

    grad_tiles(2)
    grad_tiles(3)
    text_part(quarter, half)
    for k, (way, d) in enumerate(relays):
        hstage[k] = q_ref[place(way, d + quarter)].astype(BF16)
        h_copy(k).start()
    grad_tiles(0)
    grad_tiles(1)
    text_part(0, quarter)
    for k, (way, d) in enumerate(directs):
        dstage[k] = q_ref[place(way, d)].astype(BF16)
        d_copy(k).start()

    def image_part(c):
        at = pl.ds(pl.multiple_of(c * 2 * rows, 128), 2 * rows)
        p_ref[...] = jnp.dot(text_tr[...], g_ref[:, at], preferred_element_type=F32)

    def pack(out, more, t2):
        at = pl.ds(pl.multiple_of(t2 * wx, wx), wx)
        middle = p_ref[at, 128:256]
        m1 = middle[: wx // 2]
        m2 = middle[wx // 2 :]
        parts = (
            (p_ref[at, 0:128], jnp.where(low, m1, pltpu.roll(m2, 64, 1))),
            (p_ref[at, 256:384], jnp.where(low, pltpu.roll(m1, 64, 1), m2)),
        )
        for y0, (main, rest) in enumerate(parts):
            k = stu_place(0, lax.div(t2, 2), y0, lax.rem(t2, 2))
            if more is not None:
                main = main + more[k, pl.ds(0, wx), :].astype(F32)
                rest = rest + more[k, pl.ds(wx, wx // 2), :].astype(F32)
            out[k, pl.ds(0, wx), :] = main.astype(BF16)
            out[k, pl.ds(wx, wx // 2), :] = rest.astype(BF16)

    image_part(1 - core)
    loop(0, tn, lambda t2: pack(sstage, None, t2))
    i_sib = remote(sstage, sland, send.at[7], recv.at[7], sibling)
    i_sib.start()
    image_part(core)
    i_sib.wait_recv()
    loop(0, tn, lambda t2: pack(istage, sland, t2))

    def i_copy(m):
        dx, dy = chip_at(m)
        y2 = lax.rem(y + dy, 4)
        src = istage.at[
            stu_place(0, lax.rem(x + dx, xn), lax.rem(y2, 2), lax.div(y2, 2))
        ]
        return remote(src, iland.at[m], send.at[8], recv.at[8], at_chip(dx, dy, core))

    loop(0, sn - 1, lambda m: i_copy(m).start())

    whole_of(hland, 4, len(relays)).wait_recv()
    for way in range(2):
        total = q_ref[place(way, quarter)]
        for k, (w, d) in enumerate(relays):
            if w == way:
                total = total + hland[k].astype(F32)
        fstage[way] = total.astype(BF16)
        f_copy(way).start()

    whole_of(cmean, 1, zn - 1).wait_recv()
    col_mean = join_mean(
        [cbuf[k][1:2] for k in range(zn)], [cmean[k] for k in range(zn)], col_lse[1:2]
    )
    row_mean = join_mean(
        [rbuf[k][1:2] for k in range(sn)], [rbuf[k][2:3] for k in range(sn)], row_lse[1:2]
    )
    col_loss = col_lse[0:1] - col_mean
    row_loss = row_lse[0:1] - row_mean
    own_col = pltpu.roll(jnp.broadcast_to(col_loss, (8, texts)), texts - z * pairs, 1)
    own_row = pltpu.roll(
        jnp.broadcast_to(row_loss, (8, images)), images - rb * rows - t * pairs, 1
    )
    loss_ref[...] = 0.5 * (own_col[0:1, 0:pairs] + own_row[0:1, 0:pairs])

    for c in range(2):
        some = bufs[c].at[pl.ds(0, zn - 1)]
        remote(some, some, tsend.at[c], trecv.at[c, 0, 0], sibling).wait_send()
    for k, count in ((0, 3), (1, 12), (2, sn)):
        some = stu.at[pl.ds(0, count)]
        remote(some, some, ssend.at[k], srecv.at[k], sibling).wait_send()
    teach(0, xt_ref, block(rb, 0, rows), sibling).wait_send()
    teach(1, both_far, both_far, sibling).wait_send()
    whole_of(cbuf, 0, zn - 1).wait_send()
    whole_of(cmean, 1, zn - 1).wait_send()
    r_sib.wait_send()
    whole_of(rbuf, 3, sn - 1).wait_send()
    whole_of(hstage, 4, len(relays)).wait_send()
    whole_of(dstage, 5, len(directs)).wait_send()
    i_sib.wait_send()

    whole_of(iland, 8, sn - 1).wait_recv()
    total = istage[stu_place(0, x, ylo, yhi)].astype(F32)
    for k in range(sn - 1):
        total = total + iland[k].astype(F32)
    total = total * factor_s
    main = total[:wx]
    rest = jnp.concatenate([total[wx:, :64], total[wx:, 64:]], 0)
    gi_ref[...] = jnp.where(
        odd, jnp.concatenate([rest, main], 1), jnp.concatenate([main, rest], 1)
    )
    whole_of(iland, 8, sn - 1).wait_send()

    whole_of(dland, 5, len(directs)).wait_recv()
    total = q_ref[zn - 1]
    for k in range(len(directs)):
        total = total + dland[k].astype(F32)
    whole_of(fland, 6, 2).wait_recv()
    for way in range(2):
        total = total + fland[way].astype(F32)
    gt_ref[...] = total * factor_s
    whole_of(fland, 6, 2).wait_send()


def deliver(loss_ref, image_ref, text_ref, loss_out, image_out, text_out):
    loss_out[...] = loss_ref[...]
    image_out[...] = image_ref[...]
    text_out[...] = text_ref[...]


def body(zn, tn, image_student, text_student, image_teacher, text_teacher, ss, st):
    rows = image_teacher.shape[0]
    pairs, ws = text_student.shape
    wt = text_teacher.shape[1]
    wx = ws // tn
    texts, images, half = zn * pairs, 4 * rows, zn // 2
    sn = 2 * tn
    high = wx * rows // 128
    dma = pltpu.SemaphoreType.DMA
    anywhere = pl.BlockSpec(memory_space=pl.ANY)
    vmem = pl.BlockSpec(memory_space=pltpu.VMEM)
    smem = pl.BlockSpec(memory_space=pltpu.SMEM)
    score = pltpu.VMEM((texts, images), F32)
    loss, grad_image, grad_text = pl.pallas_call(
        functools.partial(kernel, zn, tn),
        out_shape=(
            jax.ShapeDtypeStruct((1, pairs), F32),
            jax.ShapeDtypeStruct((wx, rows), F32),
            jax.ShapeDtypeStruct((pairs, ws), F32),
        ),
        in_specs=[anywhere] * 4 + [smem, smem],
        out_specs=(vmem, vmem, vmem),
        scratch_shapes=[
            pltpu.VMEM((wx, rows), BF16),
            pltpu.VMEM((zn, pairs, (ws + wt) // 2), BF16),
            pltpu.VMEM((zn, pairs, (ws + wt) // 2), BF16),
            pltpu.VMEM((texts, ws), BF16),
            pltpu.VMEM((texts, wt), BF16),
            pltpu.VMEM((ws, texts), BF16),
            pltpu.VMEM((2 * sn, high, 128), BF16),
            pltpu.VMEM((ws, images), BF16),
            pltpu.VMEM((images, wt), BF16),
            score,
            score,
            score,
            score,
            score,
            score,
            pltpu.VMEM((texts, 128), F32),
            pltpu.VMEM((zn, 2, texts), F32),
            pltpu.VMEM((zn, 1, texts), F32),
            pltpu.VMEM((sn, 4, images), F32),
            pltpu.VMEM((texts, 128), F32),
            pltpu.VMEM((texts, images), BF16),
            pltpu.VMEM((zn, pairs, ws), F32),
            pltpu.VMEM((ws, 2 * rows), F32),
            pltpu.VMEM((half - 2, pairs, ws), BF16),
            pltpu.VMEM((half - 2, pairs, ws), BF16),
            pltpu.VMEM((half - 1, pairs, ws), BF16),
            pltpu.VMEM((half - 1, pairs, ws), BF16),
            pltpu.VMEM((2, pairs, ws), BF16),
            pltpu.VMEM((2, pairs, ws), BF16),
            pltpu.VMEM((sn, high, 128), BF16),
            pltpu.VMEM((sn, high, 128), BF16),
            pltpu.VMEM((sn, high, 128), BF16),
            pltpu.VMEM((sn - 1, high, 128), BF16),
            pltpu.VMEM((2, 4, images), F32),
            dma((5,)),
            dma((2,)),
            dma((2, 2, half)),
            dma((2,)),
            dma((2,)),
            dma((3,)),
            dma((3,)),
            dma((9,)),
            dma((9,)),
        ],
        compiler_params=pltpu.CompilerParams(
            collective_id=0, has_side_effects=True, vmem_limit_bytes=62 * 2**20
        ),
    )(image_student.T, image_teacher, text_student, text_teacher, ss, st)
    loss, grad_image, grad_text = pl.pallas_call(
        deliver,
        out_shape=[jax.ShapeDtypeStruct(v.shape, F32) for v in (loss, grad_image, grad_text)],
        in_specs=[vmem] * 3,
        out_specs=[vmem] * 3,
    )(loss, grad_image, grad_text)
    return loss.reshape(pairs), grad_image.T, grad_text


def solution(mesh):
    zn = mesh.shape["batch"] // 4
    tn = mesh.shape["tensor"]
    return jax.shard_map(
        functools.partial(body, zn, tn),
        mesh=mesh,
        in_specs=(
            P("batch", "tensor"),
            P(("batch", "tensor"), None),
            P("batch", None),
            P(("batch", "tensor"), None),
            P(),
            P(),
        ),
        out_specs=(P(("batch", "tensor")), P("batch", "tensor"), P(("batch", "tensor"), None)),
        check_vma=False,
    )
```

```python
import functools

import jax
import jax.numpy as jnp
from jax import lax
from jax.experimental import pallas as pl
from jax.experimental.pallas import tpu as pltpu
from jax.sharding import PartitionSpec as P

MESH = pl.DeviceIdType.MESH
F32 = jnp.float32
BF16 = jnp.bfloat16
NN = (((1,), (0,)), ((), ()))
NT = (((1,), (1,)), ((), ()))


def remote(src, dst, send, recv, device):
    return pltpu.make_async_remote_copy(
        src_ref=src,
        dst_ref=dst,
        send_sem=send,
        recv_sem=recv,
        device_id=device,
        device_id_type=MESH,
    )


def loop(low, high, body):
    def step(i, carry):
        body(i)
        return carry

    lax.fori_loop(low, high, step, 0)


def join_lse(parts):
    peak = functools.reduce(jnp.maximum, parts)
    return peak + jnp.log(sum(jnp.exp(v - peak) for v in parts))


def join_mean(lses, means, lse):
    return sum(jnp.exp(v - lse) * m for v, m in zip(lses, means))


def kernel(
    zn,
    tn,
    xs_ref,
    xt_ref,
    ts_ref,
    tt_ref,
    ss_ref,
    st_ref,
    loss_ref,
    gi_ref,
    gt_ref,
    xs_v,
    buf_a,
    buf_b,
    text_s,
    text_t,
    text_tr,
    stu,
    img_s,
    img_t,
    sc_s,
    sc_t,
    e_rs,
    e_rt,
    e_cs,
    e_ct,
    colstat,
    cbuf,
    cmean,
    rbuf,
    rmean,
    colback,
    g_ref,
    q_ref,
    p_ref,
    dstage,
    dland,
    hstage,
    hland,
    ostage,
    oland,
    fstage,
    fland,
    sstage,
    sland,
    istage,
    iland,
    rsib,
    lsem,
    tsend,
    trecv,
    xsend,
    xrecv,
    ssend,
    srecv,
    send,
    recv,
):
    xn = tn // 2
    half = zn // 2
    b = lax.axis_index("batch")
    t = lax.axis_index("tensor")
    z = lax.div(b, 4)
    ylo = lax.rem(lax.div(b, 2), 2)
    core = lax.rem(b, 2)
    x = lax.div(t, 2)
    yhi = lax.rem(t, 2)
    y = yhi * 2 + ylo
    rb = core * 2 + ylo
    rows = xt_ref.shape[0]
    mid = rows // 2
    pairs, ws = ts_ref.shape
    wt = tt_ref.shape[1]
    wc = (ws + wt) // 2
    wa = wc - ws
    wx = ws // tn
    texts = zn * pairs
    images = 4 * rows
    tile = 2 * pairs

    def at_chip(dx, dy, c):
        x2 = lax.rem(x + dx, xn)
        y2 = lax.rem(y + dy, 4)
        return (4 * z + lax.rem(y2, 2) * 2 + c, x2 * 2 + lax.div(y2, 2))

    def ring(d):
        return (lax.rem(z + d, zn) * 4 + ylo * 2 + core, t)

    sibling = (b + 1 - 2 * core, t)
    right = ring(1)
    left = ring(zn - 1)
    near = [right, left, sibling]
    near += [at_chip(d, 0, core) for d in range(1, xn)]
    near += [at_chip(0, d, core) for d in range(1, 4)]
    barrier = pltpu.get_barrier_semaphore()
    for device in near:
        pl.semaphore_signal(barrier, inc=1, device_id=device, device_id_type=MESH)

    bufs = (buf_a, buf_b)
    texts_in = [
        pltpu.make_async_copy(ts_ref, buf_a.at[z, :, pl.ds(0, ws)], lsem.at[1]),
        pltpu.make_async_copy(
            tt_ref.at[:, pl.ds(0, wa)], buf_a.at[z, :, pl.ds(ws, wa)], lsem.at[2]
        ),
        pltpu.make_async_copy(tt_ref.at[:, pl.ds(wa, wc)], buf_b.at[z], lsem.at[3]),
    ]
    for copy in texts_in:
        copy.start()
    own_xs = pltpu.make_async_copy(xs_ref, xs_v, lsem.at[0])
    own_xs.start()

    def block(r, start, size):
        return img_t.at[pl.ds(pl.multiple_of(r * rows + start, mid), size)]

    own_xt = pltpu.make_async_copy(xt_ref, block(rb, 0, rows), lsem.at[4])
    own_xt.start()

    own_xs.wait()
    whole = xs_v[...].astype(F32)
    odd = ylo == 1
    main = jnp.where(odd, whole[:, rows - 128 :], whole[:, :128])
    rest = jnp.where(odd, whole[:, : rows - 128], whole[:, 128:])
    packed = jnp.concatenate([rest[: wx // 2], rest[wx // 2 :]], 1)

    def stu_place(c, x2, y0, y1):
        return (c * xn + x2) * 4 + y0 * 2 + y1

    own_stu = stu.at[stu_place(core, x, ylo, yhi)]
    own_stu[0:wx, :] = main.astype(BF16)
    own_stu[wx:, :] = packed.astype(BF16)

    for copy in texts_in:
        copy.wait()
    pl.semaphore_wait(barrier, len(near))

    def text_copy(c, way, s):
        o = lax.rem(z + (zn - s if way == 0 else s), zn)
        slot = bufs[c].at[o]
        return remote(
            slot, slot, tsend.at[c], trecv.at[c, way, s], right if way == 0 else left
        )

    def text_wait(c, way, s):
        o = lax.rem(z + (zn - 1 - s if way == 0 else 1 + s), zn)
        slot = bufs[c].at[o]
        remote(slot, slot, tsend.at[c], trecv.at[c, way, s], right).wait_recv()

    def text_step(s):
        for c in range(2):
            for way in range(2):
                if s > half - 1 or (way == 1 and s > half - 2):
                    text_wait(c, way, s - 1)
                else:
                    text_wait(c, way, s - 1)
                    text_copy(c, way, s).start()

    for c in range(2):
        for way in range(2):
            text_copy(c, way, 0).start()

    def stu_y(d):
        return remote(own_stu, own_stu, ssend.at[0], srecv.at[0], at_chip(0, d, core))

    for d in (2, 1, 3):
        stu_y(d).start()

    up = at_chip(0, 1, core)
    down = at_chip(0, 3, core)
    other = core * 2 + 1 - ylo
    far = (1 - core) * 2

    def teach(k, src, dst, device):
        return remote(src, dst, xsend.at[k], xrecv.at[k], device)

    to_up = teach(0, xt_ref.at[pl.ds(0, mid)], block(rb, 0, mid), up)
    to_down = teach(0, xt_ref.at[pl.ds(mid, mid)], block(rb, mid, mid), down)
    to_sib = teach(1, xt_ref, block(rb, 0, rows), sibling)
    to_up.start()
    to_down.start()
    to_sib.start()

    text_step(1)
    def stu_wait(k, count):
        some = stu.at[pl.ds(0, count)]
        remote(some, some, ssend.at[k], srecv.at[k], sibling).wait_recv()

    stu_wait(0, 3)
    own_four = stu.at[pl.ds(stu_place(core, x, 0, 0), 4)]

    def stu_x(d):
        return remote(own_four, own_four, ssend.at[1], srecv.at[1], at_chip(d, 0, core))

    for d in (2, 1, 3):
        stu_x(d).start()
    text_step(2)
    text_step(3)
    sn = 4 * xn
    teach(0, xt_ref, block(other, 0, rows), up).wait_recv()
    to_sib2 = teach(1, block(other, 0, rows), block(other, 0, rows), sibling)
    to_sib2.start()
    stu_wait(1, sn - 4)
    mine = stu.at[pl.ds(core * sn, sn)]
    stu_sib = remote(mine, mine, ssend.at[2], srecv.at[2], sibling)
    stu_sib.start()
    text_step(4)
    own_xt.wait()

    stu_wait(2, sn)
    low = lax.broadcasted_iota(jnp.int32, (wx // 2, 128), 1) < 64

    def unpack(k):
        c = lax.div(k, tn)
        t2 = lax.rem(k, tn)
        even = stu[stu_place(c, lax.div(t2, 2), 0, lax.rem(t2, 2))].astype(F32)
        odds = stu[stu_place(c, lax.div(t2, 2), 1, lax.rem(t2, 2))].astype(F32)
        e2 = even[wx:]
        o2 = odds[wx:]
        middle = jnp.concatenate(
            [jnp.where(low, e2, pltpu.roll(o2, 64, 1)), jnp.where(low, pltpu.roll(e2, 64, 1), o2)],
            0,
        )
        at = pl.ds(pl.multiple_of(t2 * wx, wx), wx)
        for k2, part in enumerate((even[:wx], middle, odds[:wx])):
            lanes = pl.ds(pl.multiple_of(c * 2 * rows + k2 * 128, 128), 128)
            img_s[at, lanes] = part.astype(BF16)

    loop(0, 2 * tn, unpack)
    both_far = img_t.at[pl.ds(pl.multiple_of(far * rows, mid), 2 * rows)]
    teach(1, both_far, both_far, sibling).wait_recv()

    factor_s = ss_ref[0] / jnp.sqrt(jnp.float32(ws))
    factor_t = st_ref[0] / jnp.sqrt(jnp.float32(wt))
    lane = lax.broadcasted_iota(jnp.int32, (tile, 128), 1)

    def owners(i):
        more = 1 - lax.div(i, half - 1)
        return lax.rem(z + zn - 1 - i, zn), lax.rem(z + (1 + i) * more, zn)

    def at_owner(o):
        return pl.ds(pl.multiple_of(o * pairs, 8), pairs)

    def fold(v, op):
        out = v[0:8]
        for k in range(1, tile // 8):
            out = op(out, v[8 * k : 8 * k + 8])
        return out

    def batch(first, end):
        last = end == half

        def at_tile(i):
            return pl.ds(pl.multiple_of(i * tile, tile), tile)

        def both(buf, i):
            o1, o2 = owners(i)
            return jnp.concatenate([buf[o1].astype(F32), buf[o2].astype(F32)], 0).astype(BF16)

        def join_a(i):
            one = both(buf_a, i)
            text_s[at_tile(i), :] = one[:, :ws]
            text_t[at_tile(i), pl.ds(0, wa)] = one[:, ws:]

        def join_b(i):
            text_t[at_tile(i), pl.ds(wa, wc)] = both(buf_b, i)

        part = pl.ds(first * tile, (end - first) * tile)

        def teacher(start, size):
            at = pl.ds(start, size)
            return lax.dot_general(
                text_t[part, at], img_t[:, at], NT, preferred_element_type=F32
            )

        if last:
            text_wait(0, 0, half - 1)
        loop(first, end, join_a)
        sc_s[part, :] = (
            lax.dot_general(text_s[part, :], img_s[...], NN, preferred_element_type=F32) * factor_s
        )
        if last:
            sc_t[part, :] = teacher(0, wa)
            text_wait(1, 0, half - 1)
        loop(first, end, join_b)
        if last:
            sc_t[part, :] = (sc_t[part, :] + teacher(wa, wc)) * factor_t
        else:
            sc_t[part, :] = teacher(0, wt) * factor_t

        def columns(i, carry):
            at = at_tile(i)
            s = sc_s[at, :]
            u = sc_t[at, :]
            ps = jnp.max(s, 1, keepdims=True)
            pt = jnp.max(u, 1, keepdims=True)
            es = jnp.exp(s - ps)
            et = jnp.exp(u - pt)
            e_cs[at, :] = es
            e_ct[at, :] = et
            sums = jnp.sum(es, 1, keepdims=True)
            sumt = jnp.sum(et, 1, keepdims=True)
            mean = jnp.sum(et * s, 1, keepdims=True) / sumt
            out = jnp.where(lane == 0, ps + jnp.log(sums), pt + jnp.log(sumt))
            out = jnp.where(lane == 2, mean, out)
            out = jnp.where(lane == 4, ps, out)
            out = jnp.where(lane == 5, pt, out)
            o1, o2 = owners(i)
            colstat[at_owner(o1), :] = out[:pairs]
            colstat[at_owner(o2), :] = out[pairs:]
            return (
                jnp.maximum(carry[0], fold(s, jnp.maximum)),
                jnp.maximum(carry[1], fold(u, jnp.maximum)),
            )

        none = jnp.full((8, images), -jnp.inf, F32)
        peaks = lax.fori_loop(first, end, columns, (none, none))
        row_ps = jnp.max(peaks[0], 0, keepdims=True)
        row_pt = jnp.max(peaks[1], 0, keepdims=True)

        def by_rows(i, carry):
            at = at_tile(i)
            s = sc_s[at, :]
            es = jnp.exp(s - row_ps)
            et = jnp.exp(sc_t[at, :] - row_pt)
            e_rs[at, :] = es
            e_rt[at, :] = et
            return (
                carry[0] + fold(es, jnp.add),
                carry[1] + fold(et, jnp.add),
                carry[2] + fold(et * s, jnp.add),
            )

        zero = jnp.zeros((8, images), F32)
        sums = lax.fori_loop(first, end, by_rows, (zero, zero, zero))
        return [row_ps, row_pt] + [jnp.sum(v, 0, keepdims=True) for v in sums]

    def ring_place(j):
        return half + (1 - 2 * lax.rem(j, 2)) * lax.div(j + 1, 2)

    def c_copy(j):
        return remote(cbuf.at[zn - 1], cbuf.at[j], send.at[0], recv.at[0], ring(ring_place(j)))

    def cm_copy(j):
        return remote(cmean.at[zn - 1], cmean.at[j], send.at[1], recv.at[1], ring(ring_place(j)))

    def whole_of(buf, k, count):
        some = buf.at[pl.ds(0, count)]
        return remote(some, some, send.at[k], recv.at[k], sibling)

    def send_columns():
        across = colstat[...].T
        cbuf[zn - 1] = across[0:2]
        cmean[zn - 1] = across[2:3]
        loop(0, zn - 1, lambda j: c_copy(j).start())

    cuts = [0, 4, 6, 8]
    text_step(5)
    stats = [batch(0, 4)]
    text_step(6)
    text_step(7)
    stats.append(batch(4, 6))
    stats.append(batch(6, 8))

    def merged(peak, total):
        top = functools.reduce(jnp.maximum, [s[peak] for s in stats])
        scaled = [jnp.exp(s[peak] - top) for s in stats]
        return top, scaled, sum(f * s[total] for f, s in zip(scaled, stats))

    top_s, _, rs = merged(0, 2)
    top_t, scaled, rt = merged(1, 3)
    rw = sum(f * s[4] for f, s in zip(scaled, stats))
    row = lax.broadcasted_iota(jnp.int32, (4, images), 0)

    def rows_of(ls, lt, mean):
        return jnp.where(row == 0, ls, jnp.where(row == 1, lt, mean))

    rsib[0] = rows_of(top_s + jnp.log(rs), top_t + jnp.log(rt), rw / rt)
    r_sib = remote(rsib.at[0], rsib.at[1], send.at[2], recv.at[2], sibling)
    r_sib.start()
    send_columns()
    r_sib.wait_recv()
    chip = [join_lse([rsib[0][k : k + 1], rsib[1][k : k + 1]]) for k in range(2)]
    chip_mean = join_mean(
        [rsib[0][1:2], rsib[1][1:2]], [rsib[0][2:3], rsib[1][2:3]], chip[1]
    )
    rbuf[sn - 1] = rows_of(chip[0], chip[1], chip_mean)[0:2]
    rmean[sn - 1] = chip_mean

    def chip_at(m):
        e = m + lax.div(m, 10)
        return lax.rem(e + 2, 4), lax.rem(lax.div(e, 4) + 2, 4)

    def r_copy(m):
        dx, dy = chip_at(m)
        return remote(rbuf.at[sn - 1], rbuf.at[m], send.at[3], recv.at[3], at_chip(dx, dy, core))

    def rm_copy(m):
        dx, dy = chip_at(m)
        device = at_chip(dx, dy, core)
        return remote(rmean.at[sn - 1], rmean.at[m], send.at[10], recv.at[10], device)

    loop(0, sn - 1, lambda m: r_copy(m).start())
    loop(0, zn - 1, lambda j: cm_copy(j).start())
    loop(0, sn - 1, lambda m: rm_copy(m).start())
    text_tr[...] = text_s[...].astype(F32).T.astype(BF16)

    whole_of(rbuf, 3, sn - 1).wait_recv()
    row_lse = join_lse([rbuf[k] for k in range(sn)])
    whole_of(cbuf, 0, zn - 1).wait_recv()
    col_lse = join_lse([cbuf[k] for k in range(zn)])
    colback[...] = jnp.concatenate([col_lse, jnp.zeros((126, texts), F32)], 0).T

    def grad_tiles(k):
        row_fs = 0.5 * jnp.exp(stats[k][0] - row_lse[0:1])
        row_ft = 0.5 * jnp.exp(stats[k][1] - row_lse[1:2])

        def grads(i, row_fs=row_fs, row_ft=row_ft):
            at = pl.ds(pl.multiple_of(i * tile, tile), tile)
            o1, o2 = owners(i)
            here = jnp.concatenate([colstat[at_owner(o1), :], colstat[at_owner(o2), :]], 0)
            lse = jnp.concatenate([colback[at_owner(o1), :], colback[at_owner(o2), :]], 0)
            fs = 0.5 * jnp.exp(here[:, 4:5] - lse[:, 0:1])
            ft = 0.5 * jnp.exp(here[:, 5:6] - lse[:, 1:2])
            g = e_rs[at, :] * row_fs - e_rt[at, :] * row_ft + e_cs[at, :] * fs - e_ct[at, :] * ft
            g_ref[at, :] = g.astype(BF16)

        loop(cuts[k], cuts[k + 1], grads)

    def text_part(first, end):
        at = pl.ds(first * tile, (end - first) * tile)
        part = lax.dot_general(g_ref[at, :], img_s[...], NT, preferred_element_type=F32)
        q_ref[2 * first : 2 * end] = part.reshape(2 * (end - first), pairs, ws)


    def place(way, d):
        return 2 * (half - 1) if d == half else 2 * (d - 1) + (1 if way == 0 else 0)

    def hop(way, d):
        return ring(d if way == 0 else zn - d)

    quarter = half // 2
    relays = [(w, d) for d in range(quarter - 1, 0, -1) for w in range(2)]
    directs = relays
    wg = ws // 2

    def h_copy(k):
        return remote(hstage.at[k], hland.at[k], send.at[4], recv.at[4], hop(*relays[k]))

    def d_copy(k):
        return remote(dstage.at[k], dland.at[k], send.at[5], recv.at[5], hop(*directs[k]))

    def o_copy(way):
        return remote(
            ostage.at[way], oland.at[way], send.at[9], recv.at[9], hop(way, quarter)
        )

    def f_copy(way):
        return remote(
            fstage.at[way], fland.at[way], send.at[6], recv.at[6], hop(way, quarter)
        )

    grad_tiles(1)
    grad_tiles(2)
    text_part(quarter, half)
    for way in range(2):
        ostage[way] = q_ref[place(way, half), :, way * wg : (way + 1) * wg].astype(BF16)
        o_copy(way).start()
    for k, (way, d) in enumerate(relays):
        hstage[k] = q_ref[place(way, d + quarter)].astype(BF16)
        h_copy(k).start()
    grad_tiles(0)

    text_part(0, quarter)
    for k, (way, d) in enumerate(directs):
        dstage[k] = q_ref[place(way, d)].astype(BF16)
        d_copy(k).start()

    def image_part(c):
        at = pl.ds(pl.multiple_of(c * 2 * rows, 128), 2 * rows)
        p_ref[...] = jnp.dot(text_tr[...], g_ref[:, at], preferred_element_type=F32)

    def pack(out, more, t2):
        at = pl.ds(pl.multiple_of(t2 * wx, wx), wx)
        middle = p_ref[at, 128:256]
        m1 = middle[: wx // 2]
        m2 = middle[wx // 2 :]
        parts = (
            (p_ref[at, 0:128], jnp.where(low, m1, pltpu.roll(m2, 64, 1))),
            (p_ref[at, 256:384], jnp.where(low, pltpu.roll(m1, 64, 1), m2)),
        )
        for y0, (main, rest) in enumerate(parts):
            k = stu_place(0, lax.div(t2, 2), y0, lax.rem(t2, 2))
            if more is not None:
                main = main + more[k, pl.ds(0, wx), :].astype(F32)
                rest = rest + more[k, pl.ds(wx, wx // 2), :].astype(F32)
            out[k, pl.ds(0, wx), :] = main.astype(BF16)
            out[k, pl.ds(wx, wx // 2), :] = rest.astype(BF16)

    image_part(1 - core)
    loop(0, tn, lambda t2: pack(sstage, None, t2))
    i_sib = remote(sstage, sland, send.at[7], recv.at[7], sibling)
    i_sib.start()
    image_part(core)
    i_sib.wait_recv()
    loop(0, tn, lambda t2: pack(istage, sland, t2))

    def i_copy(m):
        dx, dy = chip_at(m)
        y2 = lax.rem(y + dy, 4)
        src = istage.at[
            stu_place(0, lax.rem(x + dx, xn), lax.rem(y2, 2), lax.div(y2, 2))
        ]
        return remote(src, iland.at[m], send.at[8], recv.at[8], at_chip(dx, dy, core))

    loop(0, sn - 1, lambda m: i_copy(m).start())

    whole_of(hland, 4, len(relays)).wait_recv()
    whole_of(oland, 9, 2).wait_recv()
    for way in range(2):
        total = q_ref[place(way, quarter)]
        for k, (w, d) in enumerate(relays):
            if w == way:
                total = total + hland[k].astype(F32)
        farthest = oland[way].astype(F32)
        zero = jnp.zeros((pairs, wg), F32)
        total = total + jnp.concatenate([farthest, zero] if way == 0 else [zero, farthest], 1)
        fstage[way] = total.astype(BF16)
        f_copy(way).start()

    whole_of(cmean, 1, zn - 1).wait_recv()
    whole_of(rmean, 10, sn - 1).wait_recv()
    col_mean = join_mean(
        [cbuf[k][1:2] for k in range(zn)], [cmean[k] for k in range(zn)], col_lse[1:2]
    )
    row_mean = join_mean(
        [rbuf[k][1:2] for k in range(sn)], [rmean[k] for k in range(sn)], row_lse[1:2]
    )
    col_loss = col_lse[0:1] - col_mean
    row_loss = row_lse[0:1] - row_mean
    own_col = pltpu.roll(jnp.broadcast_to(col_loss, (8, texts)), texts - z * pairs, 1)
    own_row = pltpu.roll(
        jnp.broadcast_to(row_loss, (8, images)), images - rb * rows - t * pairs, 1
    )
    loss_ref[...] = 0.5 * (own_col[0:1, 0:pairs] + own_row[0:1, 0:pairs])

    for c in range(2):
        some = bufs[c].at[pl.ds(0, zn - 1)]
        remote(some, some, tsend.at[c], trecv.at[c, 0, 0], sibling).wait_send()
    for k, count in ((0, 3), (1, 12), (2, sn)):
        some = stu.at[pl.ds(0, count)]
        remote(some, some, ssend.at[k], srecv.at[k], sibling).wait_send()
    teach(0, xt_ref, block(rb, 0, rows), sibling).wait_send()
    teach(1, both_far, both_far, sibling).wait_send()
    whole_of(cbuf, 0, zn - 1).wait_send()
    whole_of(cmean, 1, zn - 1).wait_send()
    r_sib.wait_send()
    whole_of(rbuf, 3, sn - 1).wait_send()
    whole_of(rmean, 10, sn - 1).wait_send()
    whole_of(hstage, 4, len(relays)).wait_send()
    whole_of(ostage, 9, 2).wait_send()
    whole_of(dstage, 5, len(directs)).wait_send()
    i_sib.wait_send()

    whole_of(iland, 8, sn - 1).wait_recv()
    total = istage[stu_place(0, x, ylo, yhi)].astype(F32)
    for k in range(sn - 1):
        total = total + iland[k].astype(F32)
    total = total * factor_s
    main = total[:wx]
    rest = jnp.concatenate([total[wx:, :64], total[wx:, 64:]], 0)
    gi_ref[...] = jnp.where(
        odd, jnp.concatenate([rest, main], 1), jnp.concatenate([main, rest], 1)
    )
    whole_of(iland, 8, sn - 1).wait_send()

    whole_of(dland, 5, len(directs)).wait_recv()
    total = q_ref[zn - 1]
    for k in range(len(directs)):
        total = total + dland[k].astype(F32)
    whole_of(fland, 6, 2).wait_recv()
    for way in range(2):
        total = total + fland[way].astype(F32)
    gt_ref[...] = total * factor_s
    whole_of(fland, 6, 2).wait_send()


def deliver(loss_ref, image_ref, text_ref, loss_out, image_out, text_out):
    loss_out[...] = loss_ref[...]
    image_out[...] = image_ref[...]
    text_out[...] = text_ref[...]


def body(zn, tn, image_student, text_student, image_teacher, text_teacher, ss, st):
    rows = image_teacher.shape[0]
    pairs, ws = text_student.shape
    wt = text_teacher.shape[1]
    wx = ws // tn
    texts, images, half = zn * pairs, 4 * rows, zn // 2
    sn = 2 * tn
    high = wx * rows // 128
    dma = pltpu.SemaphoreType.DMA
    anywhere = pl.BlockSpec(memory_space=pl.ANY)
    vmem = pl.BlockSpec(memory_space=pltpu.VMEM)
    smem = pl.BlockSpec(memory_space=pltpu.SMEM)
    score = pltpu.VMEM((texts, images), F32)
    loss, grad_image, grad_text = pl.pallas_call(
        functools.partial(kernel, zn, tn),
        out_shape=(
            jax.ShapeDtypeStruct((1, pairs), F32),
            jax.ShapeDtypeStruct((wx, rows), F32),
            jax.ShapeDtypeStruct((pairs, ws), F32),
        ),
        in_specs=[anywhere] * 4 + [smem, smem],
        out_specs=(vmem, vmem, vmem),
        scratch_shapes=[
            pltpu.VMEM((wx, rows), BF16),
            pltpu.VMEM((zn, pairs, (ws + wt) // 2), BF16),
            pltpu.VMEM((zn, pairs, (ws + wt) // 2), BF16),
            pltpu.VMEM((texts, ws), BF16),
            pltpu.VMEM((texts, wt), BF16),
            pltpu.VMEM((ws, texts), BF16),
            pltpu.VMEM((2 * sn, high, 128), BF16),
            pltpu.VMEM((ws, images), BF16),
            pltpu.VMEM((images, wt), BF16),
            score,
            score,
            score,
            score,
            score,
            score,
            pltpu.VMEM((texts, 128), F32),
            pltpu.VMEM((zn, 2, texts), F32),
            pltpu.VMEM((zn, 1, texts), F32),
            pltpu.VMEM((sn, 2, images), F32),
            pltpu.VMEM((sn, 1, images), F32),
            pltpu.VMEM((texts, 128), F32),
            pltpu.VMEM((texts, images), BF16),
            pltpu.VMEM((zn, pairs, ws), F32),
            pltpu.VMEM((ws, 2 * rows), F32),
            pltpu.VMEM((half - 2, pairs, ws), BF16),
            pltpu.VMEM((half - 2, pairs, ws), BF16),
            pltpu.VMEM((half - 2, pairs, ws), BF16),
            pltpu.VMEM((half - 2, pairs, ws), BF16),
            pltpu.VMEM((2, pairs, ws // 2), BF16),
            pltpu.VMEM((2, pairs, ws // 2), BF16),
            pltpu.VMEM((2, pairs, ws), BF16),
            pltpu.VMEM((2, pairs, ws), BF16),
            pltpu.VMEM((sn, high, 128), BF16),
            pltpu.VMEM((sn, high, 128), BF16),
            pltpu.VMEM((sn, high, 128), BF16),
            pltpu.VMEM((sn - 1, high, 128), BF16),
            pltpu.VMEM((2, 4, images), F32),
            dma((5,)),
            dma((2,)),
            dma((2, 2, half)),
            dma((2,)),
            dma((2,)),
            dma((3,)),
            dma((3,)),
            dma((11,)),
            dma((11,)),
        ],
        compiler_params=pltpu.CompilerParams(
            collective_id=0, has_side_effects=True, vmem_limit_bytes=62 * 2**20
        ),
    )(image_student.T, image_teacher, text_student, text_teacher, ss, st)
    loss, grad_image, grad_text = pl.pallas_call(
        deliver,
        out_shape=[jax.ShapeDtypeStruct(v.shape, F32) for v in (loss, grad_image, grad_text)],
        in_specs=[vmem] * 3,
        out_specs=[vmem] * 3,
    )(loss, grad_image, grad_text)
    return loss.reshape(pairs), grad_image.T, grad_text


def solution(mesh):
    zn = mesh.shape["batch"] // 4
    tn = mesh.shape["tensor"]
    return jax.shard_map(
        functools.partial(body, zn, tn),
        mesh=mesh,
        in_specs=(
            P("batch", "tensor"),
            P(("batch", "tensor"), None),
            P("batch", None),
            P(("batch", "tensor"), None),
            P(),
            P(),
        ),
        out_specs=(P(("batch", "tensor")), P("batch", "tensor"), P(("batch", "tensor"), None)),
        check_vma=False,
    )
```

```python
import functools

import jax
import jax.numpy as jnp
from jax import lax
from jax.experimental import pallas as pl
from jax.experimental.pallas import tpu as pltpu
from jax.sharding import PartitionSpec as P

MESH = pl.DeviceIdType.MESH
F32 = jnp.float32
BF16 = jnp.bfloat16
NN = (((1,), (0,)), ((), ()))
NT = (((1,), (1,)), ((), ()))


def remote(src, dst, send, recv, device):
    return pltpu.make_async_remote_copy(
        src_ref=src,
        dst_ref=dst,
        send_sem=send,
        recv_sem=recv,
        device_id=device,
        device_id_type=MESH,
    )


def loop(low, high, body, unroll=False):
    def step(i, carry):
        body(i)
        return carry

    lax.fori_loop(low, high, step, 0, unroll=unroll)


def join_lse(parts):
    peak = functools.reduce(jnp.maximum, parts)
    return peak + jnp.log(sum(jnp.exp(v - peak) for v in parts))


def join_mean(lses, means, lse):
    return sum(jnp.exp(v - lse) * m for v, m in zip(lses, means))


def kernel(
    zn,
    tn,
    xs_ref,
    xt_ref,
    ts_ref,
    tt_ref,
    ss_ref,
    st_ref,
    loss_ref,
    gi_ref,
    gt_ref,
    xs_v,
    buf_a,
    buf_b,
    text_s,
    text_t,
    text_tr,
    stu,
    img_s,
    img_t,
    sc_s,
    sc_t,
    e_rs,
    e_rt,
    e_cs,
    e_ct,
    colstat,
    cbuf,
    cmean,
    rbuf,
    rmean,
    colback,
    g_ref,
    q_ref,
    p_ref,
    dstage,
    dland,
    hstage,
    hland,
    ostage,
    oland,
    fstage,
    fland,
    sstage,
    sland,
    istage,
    iland,
    rsib,
    lsem,
    tsend,
    trecv,
    xsend,
    xrecv,
    ssend,
    srecv,
    send,
    recv,
):
    xn = tn // 2
    half = zn // 2
    b = lax.axis_index("batch")
    t = lax.axis_index("tensor")
    z = lax.div(b, 4)
    ylo = lax.rem(lax.div(b, 2), 2)
    core = lax.rem(b, 2)
    x = lax.div(t, 2)
    yhi = lax.rem(t, 2)
    y = yhi * 2 + ylo
    rb = core * 2 + ylo
    rows = xt_ref.shape[0]
    mid = rows // 2
    pairs, ws = ts_ref.shape
    wt = tt_ref.shape[1]
    wc = (ws + wt) // 2
    wa = wc - ws
    wx = ws // tn
    texts = zn * pairs
    images = 4 * rows
    tile = 2 * pairs

    def at_chip(dx, dy, c):
        x2 = lax.rem(x + dx, xn)
        y2 = lax.rem(y + dy, 4)
        return (4 * z + lax.rem(y2, 2) * 2 + c, x2 * 2 + lax.div(y2, 2))

    def ring(d):
        return (lax.rem(z + d, zn) * 4 + ylo * 2 + core, t)

    sibling = (b + 1 - 2 * core, t)
    right = ring(1)
    left = ring(zn - 1)
    near = [right, left, sibling]
    near += [at_chip(d, 0, core) for d in range(1, xn)]
    near += [at_chip(0, d, core) for d in range(1, 4)]
    barrier = pltpu.get_barrier_semaphore()
    for device in near:
        pl.semaphore_signal(barrier, inc=1, device_id=device, device_id_type=MESH)

    bufs = (buf_a, buf_b)
    texts_in = [
        pltpu.make_async_copy(ts_ref, buf_a.at[z, :, pl.ds(0, ws)], lsem.at[1]),
        pltpu.make_async_copy(
            tt_ref.at[:, pl.ds(0, wa)], buf_a.at[z, :, pl.ds(ws, wa)], lsem.at[2]
        ),
        pltpu.make_async_copy(tt_ref.at[:, pl.ds(wa, wc)], buf_b.at[z], lsem.at[3]),
    ]
    for copy in texts_in:
        copy.start()
    own_xs = pltpu.make_async_copy(xs_ref, xs_v, lsem.at[0])
    own_xs.start()

    def block(r, start, size):
        return img_t.at[pl.ds(pl.multiple_of(r * rows + start, mid), size)]

    own_xt = pltpu.make_async_copy(xt_ref, block(rb, 0, rows), lsem.at[4])
    own_xt.start()

    own_xs.wait()
    whole = xs_v[...].astype(F32)
    odd = ylo == 1
    main = jnp.where(odd, whole[:, rows - 128 :], whole[:, :128])
    rest = jnp.where(odd, whole[:, : rows - 128], whole[:, 128:])
    packed = jnp.concatenate([rest[: wx // 2], rest[wx // 2 :]], 1)

    def stu_place(c, x2, y0, y1):
        return (c * xn + x2) * 4 + y0 * 2 + y1

    own_stu = stu.at[stu_place(core, x, ylo, yhi)]
    own_stu[0:wx, :] = main.astype(BF16)
    own_stu[wx:, :] = packed.astype(BF16)

    for copy in texts_in:
        copy.wait()
    pl.semaphore_wait(barrier, len(near))

    def text_copy(c, way, s):
        o = lax.rem(z + (zn - s if way == 0 else s), zn)
        slot = bufs[c].at[o]
        return remote(
            slot, slot, tsend.at[c], trecv.at[c, way, s], right if way == 0 else left
        )

    def text_wait(c, way, s):
        o = lax.rem(z + (zn - 1 - s if way == 0 else 1 + s), zn)
        slot = bufs[c].at[o]
        remote(slot, slot, tsend.at[c], trecv.at[c, way, s], right).wait_recv()

    def text_step(s):
        for c in range(2):
            for way in range(2):
                if s > half - 1 or (way == 1 and s > half - 2):
                    text_wait(c, way, s - 1)
                else:
                    text_wait(c, way, s - 1)
                    text_copy(c, way, s).start()

    for c in range(2):
        for way in range(2):
            text_copy(c, way, 0).start()

    def stu_y(d):
        return remote(own_stu, own_stu, ssend.at[0], srecv.at[0], at_chip(0, d, core))

    for d in (2, 1, 3):
        stu_y(d).start()

    up = at_chip(0, 1, core)
    down = at_chip(0, 3, core)
    other = core * 2 + 1 - ylo
    far = (1 - core) * 2

    def teach(k, src, dst, device):
        return remote(src, dst, xsend.at[k], xrecv.at[k], device)

    to_up = teach(0, xt_ref.at[pl.ds(0, mid)], block(rb, 0, mid), up)
    to_down = teach(0, xt_ref.at[pl.ds(mid, mid)], block(rb, mid, mid), down)
    to_sib = teach(1, xt_ref, block(rb, 0, rows), sibling)
    to_up.start()
    to_down.start()
    to_sib.start()

    text_step(1)
    def stu_wait(k, count):
        some = stu.at[pl.ds(0, count)]
        remote(some, some, ssend.at[k], srecv.at[k], sibling).wait_recv()

    stu_wait(0, 3)
    own_four = stu.at[pl.ds(stu_place(core, x, 0, 0), 4)]

    def stu_x(d):
        return remote(own_four, own_four, ssend.at[1], srecv.at[1], at_chip(d, 0, core))

    for d in (2, 1, 3):
        stu_x(d).start()
    text_step(2)
    text_step(3)
    sn = 4 * xn
    teach(0, xt_ref, block(other, 0, rows), up).wait_recv()
    to_sib2 = teach(1, block(other, 0, rows), block(other, 0, rows), sibling)
    to_sib2.start()
    stu_wait(1, sn - 4)
    mine = stu.at[pl.ds(core * sn, sn)]
    stu_sib = remote(mine, mine, ssend.at[2], srecv.at[2], sibling)
    stu_sib.start()
    text_step(4)
    own_xt.wait()

    stu_wait(2, sn)
    low = lax.broadcasted_iota(jnp.int32, (wx // 2, 128), 1) < 64

    def unpack(k):
        c = lax.div(k, tn)
        t2 = lax.rem(k, tn)
        even = stu[stu_place(c, lax.div(t2, 2), 0, lax.rem(t2, 2))].astype(F32)
        odds = stu[stu_place(c, lax.div(t2, 2), 1, lax.rem(t2, 2))].astype(F32)
        e2 = even[wx:]
        o2 = odds[wx:]
        middle = jnp.concatenate(
            [jnp.where(low, e2, pltpu.roll(o2, 64, 1)), jnp.where(low, pltpu.roll(e2, 64, 1), o2)],
            0,
        )
        at = pl.ds(pl.multiple_of(t2 * wx, wx), wx)
        for k2, part in enumerate((even[:wx], middle, odds[:wx])):
            lanes = pl.ds(pl.multiple_of(c * 2 * rows + k2 * 128, 128), 128)
            img_s[at, lanes] = part.astype(BF16)

    loop(0, 2 * tn, unpack, True)
    both_far = img_t.at[pl.ds(pl.multiple_of(far * rows, mid), 2 * rows)]
    teach(1, both_far, both_far, sibling).wait_recv()

    factor_s = ss_ref[0] / jnp.sqrt(jnp.float32(ws))
    factor_t = st_ref[0] / jnp.sqrt(jnp.float32(wt))
    lane = lax.broadcasted_iota(jnp.int32, (tile, 128), 1)

    def owners(i):
        more = 1 - lax.div(i, half - 1)
        return lax.rem(z + zn - 1 - i, zn), lax.rem(z + (1 + i) * more, zn)

    def at_owner(o):
        return pl.ds(pl.multiple_of(o * pairs, 8), pairs)

    def fold(v, op):
        out = v[0:8]
        for k in range(1, tile // 8):
            out = op(out, v[8 * k : 8 * k + 8])
        return out

    def batch(first, end):
        last = end == half

        def at_tile(i):
            return pl.ds(pl.multiple_of(i * tile, tile), tile)

        def both(buf, i):
            o1, o2 = owners(i)
            return jnp.concatenate([buf[o1].astype(F32), buf[o2].astype(F32)], 0).astype(BF16)

        def join_a(i):
            one = both(buf_a, i)
            text_s[at_tile(i), :] = one[:, :ws]
            text_t[at_tile(i), pl.ds(0, wa)] = one[:, ws:]

        def join_b(i):
            text_t[at_tile(i), pl.ds(wa, wc)] = both(buf_b, i)

        part = pl.ds(first * tile, (end - first) * tile)

        def teacher(start, size):
            at = pl.ds(start, size)
            return lax.dot_general(
                text_t[part, at], img_t[:, at], NT, preferred_element_type=F32
            )

        if last:
            text_wait(0, 0, half - 1)
        loop(first, end, join_a, True)
        sc_s[part, :] = (
            lax.dot_general(text_s[part, :], img_s[...], NN, preferred_element_type=F32) * factor_s
        )
        if last:
            sc_t[part, :] = teacher(0, wa)
            text_wait(1, 0, half - 1)
        loop(first, end, join_b, True)
        if last:
            sc_t[part, :] = (sc_t[part, :] + teacher(wa, wc)) * factor_t
        else:
            sc_t[part, :] = teacher(0, wt) * factor_t

        def columns(i, carry):
            at = at_tile(i)
            s = sc_s[at, :]
            u = sc_t[at, :]
            ps = jnp.max(s, 1, keepdims=True)
            pt = jnp.max(u, 1, keepdims=True)
            es = jnp.exp(s - ps)
            et = jnp.exp(u - pt)
            e_cs[at, :] = es
            e_ct[at, :] = et
            sums = jnp.sum(es, 1, keepdims=True)
            sumt = jnp.sum(et, 1, keepdims=True)
            mean = jnp.sum(et * s, 1, keepdims=True) / sumt
            out = jnp.where(lane == 0, ps + jnp.log(sums), pt + jnp.log(sumt))
            out = jnp.where(lane == 2, mean, out)
            out = jnp.where(lane == 4, ps, out)
            out = jnp.where(lane == 5, pt, out)
            o1, o2 = owners(i)
            colstat[at_owner(o1), :] = out[:pairs]
            colstat[at_owner(o2), :] = out[pairs:]
            return (
                jnp.maximum(carry[0], fold(s, jnp.maximum)),
                jnp.maximum(carry[1], fold(u, jnp.maximum)),
            )

        none = jnp.full((8, images), -jnp.inf, F32)
        peaks = lax.fori_loop(first, end, columns, (none, none), unroll=True)
        row_ps = jnp.max(peaks[0], 0, keepdims=True)
        row_pt = jnp.max(peaks[1], 0, keepdims=True)

        def by_rows(i, carry):
            at = at_tile(i)
            s = sc_s[at, :]
            es = jnp.exp(s - row_ps)
            et = jnp.exp(sc_t[at, :] - row_pt)
            e_rs[at, :] = es
            e_rt[at, :] = et
            return (
                carry[0] + fold(es, jnp.add),
                carry[1] + fold(et, jnp.add),
                carry[2] + fold(et * s, jnp.add),
            )

        zero = jnp.zeros((8, images), F32)
        sums = lax.fori_loop(first, end, by_rows, (zero, zero, zero), unroll=True)
        return [row_ps, row_pt] + [jnp.sum(v, 0, keepdims=True) for v in sums]

    def ring_place(j):
        return half + (1 - 2 * lax.rem(j, 2)) * lax.div(j + 1, 2)

    def c_copy(j):
        return remote(cbuf.at[zn - 1], cbuf.at[j], send.at[0], recv.at[0], ring(ring_place(j)))

    def cm_copy(j):
        return remote(cmean.at[zn - 1], cmean.at[j], send.at[1], recv.at[1], ring(ring_place(j)))

    def whole_of(buf, k, count):
        some = buf.at[pl.ds(0, count)]
        return remote(some, some, send.at[k], recv.at[k], sibling)

    def send_columns():
        across = colstat[...].T
        cbuf[zn - 1] = across[0:2]
        cmean[zn - 1] = across[2:3]
        loop(0, zn - 1, lambda j: c_copy(j).start(), True)

    cuts = [0, 4, 6, 8]
    text_step(5)
    stats = [batch(0, 4)]
    text_step(6)
    text_step(7)
    stats.append(batch(4, 6))
    stats.append(batch(6, 8))

    def merged(peak, total):
        top = functools.reduce(jnp.maximum, [s[peak] for s in stats])
        scaled = [jnp.exp(s[peak] - top) for s in stats]
        return top, scaled, sum(f * s[total] for f, s in zip(scaled, stats))

    top_s, _, rs = merged(0, 2)
    top_t, scaled, rt = merged(1, 3)
    rw = sum(f * s[4] for f, s in zip(scaled, stats))
    row = lax.broadcasted_iota(jnp.int32, (4, images), 0)

    def rows_of(ls, lt, mean):
        return jnp.where(row == 0, ls, jnp.where(row == 1, lt, mean))

    rsib[0] = rows_of(top_s + jnp.log(rs), top_t + jnp.log(rt), rw / rt)
    r_sib = remote(rsib.at[0], rsib.at[1], send.at[2], recv.at[2], sibling)
    r_sib.start()
    send_columns()
    r_sib.wait_recv()
    chip = [join_lse([rsib[0][k : k + 1], rsib[1][k : k + 1]]) for k in range(2)]
    chip_mean = join_mean(
        [rsib[0][1:2], rsib[1][1:2]], [rsib[0][2:3], rsib[1][2:3]], chip[1]
    )
    rbuf[sn - 1] = rows_of(chip[0], chip[1], chip_mean)[0:2]
    rmean[sn - 1] = chip_mean

    def chip_at(m):
        e = m + lax.div(m, 10)
        return lax.rem(e + 2, 4), lax.rem(lax.div(e, 4) + 2, 4)

    def r_copy(m):
        dx, dy = chip_at(m)
        return remote(rbuf.at[sn - 1], rbuf.at[m], send.at[3], recv.at[3], at_chip(dx, dy, core))

    def rm_copy(m):
        dx, dy = chip_at(m)
        device = at_chip(dx, dy, core)
        return remote(rmean.at[sn - 1], rmean.at[m], send.at[10], recv.at[10], device)

    loop(0, sn - 1, lambda m: r_copy(m).start(), True)
    loop(0, zn - 1, lambda j: cm_copy(j).start(), True)
    loop(0, sn - 1, lambda m: rm_copy(m).start(), True)
    text_tr[...] = text_s[...].astype(F32).T.astype(BF16)

    whole_of(rbuf, 3, sn - 1).wait_recv()
    row_lse = join_lse([rbuf[k] for k in range(sn)])
    whole_of(cbuf, 0, zn - 1).wait_recv()
    col_lse = join_lse([cbuf[k] for k in range(zn)])
    colback[...] = jnp.concatenate([col_lse, jnp.zeros((126, texts), F32)], 0).T

    def grad_tiles(k):
        row_fs = 0.5 * jnp.exp(stats[k][0] - row_lse[0:1])
        row_ft = 0.5 * jnp.exp(stats[k][1] - row_lse[1:2])

        def grads(i, row_fs=row_fs, row_ft=row_ft):
            at = pl.ds(pl.multiple_of(i * tile, tile), tile)
            o1, o2 = owners(i)
            here = jnp.concatenate([colstat[at_owner(o1), :], colstat[at_owner(o2), :]], 0)
            lse = jnp.concatenate([colback[at_owner(o1), :], colback[at_owner(o2), :]], 0)
            fs = 0.5 * jnp.exp(here[:, 4:5] - lse[:, 0:1])
            ft = 0.5 * jnp.exp(here[:, 5:6] - lse[:, 1:2])
            g = e_rs[at, :] * row_fs - e_rt[at, :] * row_ft + e_cs[at, :] * fs - e_ct[at, :] * ft
            g_ref[at, :] = g.astype(BF16)

        loop(cuts[k], cuts[k + 1], grads, True)

    def text_part(first, end):
        at = pl.ds(first * tile, (end - first) * tile)
        part = lax.dot_general(g_ref[at, :], img_s[...], NT, preferred_element_type=F32)
        q_ref[2 * first : 2 * end] = part.reshape(2 * (end - first), pairs, ws)


    def place(way, d):
        return 2 * (half - 1) if d == half else 2 * (d - 1) + (1 if way == 0 else 0)

    def hop(way, d):
        return ring(d if way == 0 else zn - d)

    quarter = half // 2
    relays = [(w, d) for d in range(quarter - 1, 0, -1) for w in range(2)]
    directs = relays
    wg = ws // 2

    def h_copy(k):
        return remote(hstage.at[k], hland.at[k], send.at[4], recv.at[4], hop(*relays[k]))

    def d_copy(k):
        return remote(dstage.at[k], dland.at[k], send.at[5], recv.at[5], hop(*directs[k]))

    def o_copy(way):
        return remote(
            ostage.at[way], oland.at[way], send.at[9], recv.at[9], hop(way, quarter)
        )

    def f_copy(way):
        return remote(
            fstage.at[way], fland.at[way], send.at[6], recv.at[6], hop(way, quarter)
        )

    grad_tiles(1)
    grad_tiles(2)
    text_part(quarter, half)
    for way in range(2):
        ostage[way] = q_ref[place(way, half), :, way * wg : (way + 1) * wg].astype(BF16)
        o_copy(way).start()
    for k, (way, d) in enumerate(relays):
        hstage[k] = q_ref[place(way, d + quarter)].astype(BF16)
        h_copy(k).start()
    grad_tiles(0)

    text_part(0, quarter)
    for k, (way, d) in enumerate(directs):
        dstage[k] = q_ref[place(way, d)].astype(BF16)
        d_copy(k).start()

    def image_part(c):
        at = pl.ds(pl.multiple_of(c * 2 * rows, 128), 2 * rows)
        p_ref[...] = jnp.dot(text_tr[...], g_ref[:, at], preferred_element_type=F32)

    def pack(out, more, t2):
        at = pl.ds(pl.multiple_of(t2 * wx, wx), wx)
        middle = p_ref[at, 128:256]
        m1 = middle[: wx // 2]
        m2 = middle[wx // 2 :]
        parts = (
            (p_ref[at, 0:128], jnp.where(low, m1, pltpu.roll(m2, 64, 1))),
            (p_ref[at, 256:384], jnp.where(low, pltpu.roll(m1, 64, 1), m2)),
        )
        for y0, (main, rest) in enumerate(parts):
            k = stu_place(0, lax.div(t2, 2), y0, lax.rem(t2, 2))
            if more is not None:
                main = main + more[k, pl.ds(0, wx), :].astype(F32)
                rest = rest + more[k, pl.ds(wx, wx // 2), :].astype(F32)
            out[k, pl.ds(0, wx), :] = main.astype(BF16)
            out[k, pl.ds(wx, wx // 2), :] = rest.astype(BF16)

    image_part(1 - core)
    loop(0, tn, lambda t2: pack(sstage, None, t2), True)
    i_sib = remote(sstage, sland, send.at[7], recv.at[7], sibling)
    i_sib.start()
    image_part(core)
    i_sib.wait_recv()
    loop(0, tn, lambda t2: pack(istage, sland, t2), True)

    def i_copy(m):
        dx, dy = chip_at(m)
        y2 = lax.rem(y + dy, 4)
        src = istage.at[
            stu_place(0, lax.rem(x + dx, xn), lax.rem(y2, 2), lax.div(y2, 2))
        ]
        return remote(src, iland.at[m], send.at[8], recv.at[8], at_chip(dx, dy, core))

    loop(0, sn - 1, lambda m: i_copy(m).start(), True)

    whole_of(hland, 4, len(relays)).wait_recv()
    whole_of(oland, 9, 2).wait_recv()
    for way in range(2):
        total = q_ref[place(way, quarter)]
        for k, (w, d) in enumerate(relays):
            if w == way:
                total = total + hland[k].astype(F32)
        farthest = oland[way].astype(F32)
        zero = jnp.zeros((pairs, wg), F32)
        total = total + jnp.concatenate([farthest, zero] if way == 0 else [zero, farthest], 1)
        fstage[way] = total.astype(BF16)
        f_copy(way).start()

    whole_of(cmean, 1, zn - 1).wait_recv()
    whole_of(rmean, 10, sn - 1).wait_recv()
    col_mean = join_mean(
        [cbuf[k][1:2] for k in range(zn)], [cmean[k] for k in range(zn)], col_lse[1:2]
    )
    row_mean = join_mean(
        [rbuf[k][1:2] for k in range(sn)], [rmean[k] for k in range(sn)], row_lse[1:2]
    )
    col_loss = col_lse[0:1] - col_mean
    row_loss = row_lse[0:1] - row_mean
    own_col = pltpu.roll(jnp.broadcast_to(col_loss, (8, texts)), texts - z * pairs, 1)
    own_row = pltpu.roll(
        jnp.broadcast_to(row_loss, (8, images)), images - rb * rows - t * pairs, 1
    )
    loss_ref[...] = 0.5 * (own_col[0:1, 0:pairs] + own_row[0:1, 0:pairs])

    for c in range(2):
        some = bufs[c].at[pl.ds(0, zn - 1)]
        remote(some, some, tsend.at[c], trecv.at[c, 0, 0], sibling).wait_send()
    for k, count in ((0, 3), (1, 12), (2, sn)):
        some = stu.at[pl.ds(0, count)]
        remote(some, some, ssend.at[k], srecv.at[k], sibling).wait_send()
    teach(0, xt_ref, block(rb, 0, rows), sibling).wait_send()
    teach(1, both_far, both_far, sibling).wait_send()
    whole_of(cbuf, 0, zn - 1).wait_send()
    whole_of(cmean, 1, zn - 1).wait_send()
    r_sib.wait_send()
    whole_of(rbuf, 3, sn - 1).wait_send()
    whole_of(rmean, 10, sn - 1).wait_send()
    whole_of(hstage, 4, len(relays)).wait_send()
    whole_of(ostage, 9, 2).wait_send()
    whole_of(dstage, 5, len(directs)).wait_send()
    i_sib.wait_send()

    whole_of(iland, 8, sn - 1).wait_recv()
    total = istage[stu_place(0, x, ylo, yhi)].astype(F32)
    for k in range(sn - 1):
        total = total + iland[k].astype(F32)
    total = total * factor_s
    main = total[:wx]
    rest = jnp.concatenate([total[wx:, :64], total[wx:, 64:]], 0)
    gi_ref[...] = jnp.where(
        odd, jnp.concatenate([rest, main], 1), jnp.concatenate([main, rest], 1)
    )
    whole_of(iland, 8, sn - 1).wait_send()

    whole_of(dland, 5, len(directs)).wait_recv()
    total = q_ref[zn - 1]
    for k in range(len(directs)):
        total = total + dland[k].astype(F32)
    whole_of(fland, 6, 2).wait_recv()
    for way in range(2):
        total = total + fland[way].astype(F32)
    gt_ref[...] = total * factor_s
    whole_of(fland, 6, 2).wait_send()


def deliver(loss_ref, image_ref, text_ref, loss_out, image_out, text_out):
    loss_out[...] = loss_ref[...]
    image_out[...] = image_ref[...]
    text_out[...] = text_ref[...]


def body(zn, tn, image_student, text_student, image_teacher, text_teacher, ss, st):
    rows = image_teacher.shape[0]
    pairs, ws = text_student.shape
    wt = text_teacher.shape[1]
    wx = ws // tn
    texts, images, half = zn * pairs, 4 * rows, zn // 2
    sn = 2 * tn
    high = wx * rows // 128
    dma = pltpu.SemaphoreType.DMA
    anywhere = pl.BlockSpec(memory_space=pl.ANY)
    vmem = pl.BlockSpec(memory_space=pltpu.VMEM)
    smem = pl.BlockSpec(memory_space=pltpu.SMEM)
    score = pltpu.VMEM((texts, images), F32)
    loss, grad_image, grad_text = pl.pallas_call(
        functools.partial(kernel, zn, tn),
        out_shape=(
            jax.ShapeDtypeStruct((1, pairs), F32),
            jax.ShapeDtypeStruct((wx, rows), F32),
            jax.ShapeDtypeStruct((pairs, ws), F32),
        ),
        in_specs=[anywhere] * 4 + [smem, smem],
        out_specs=(vmem, vmem, vmem),
        scratch_shapes=[
            pltpu.VMEM((wx, rows), BF16),
            pltpu.VMEM((zn, pairs, (ws + wt) // 2), BF16),
            pltpu.VMEM((zn, pairs, (ws + wt) // 2), BF16),
            pltpu.VMEM((texts, ws), BF16),
            pltpu.VMEM((texts, wt), BF16),
            pltpu.VMEM((ws, texts), BF16),
            pltpu.VMEM((2 * sn, high, 128), BF16),
            pltpu.VMEM((ws, images), BF16),
            pltpu.VMEM((images, wt), BF16),
            score,
            score,
            score,
            score,
            score,
            score,
            pltpu.VMEM((texts, 128), F32),
            pltpu.VMEM((zn, 2, texts), F32),
            pltpu.VMEM((zn, 1, texts), F32),
            pltpu.VMEM((sn, 2, images), F32),
            pltpu.VMEM((sn, 1, images), F32),
            pltpu.VMEM((texts, 128), F32),
            pltpu.VMEM((texts, images), BF16),
            pltpu.VMEM((zn, pairs, ws), F32),
            pltpu.VMEM((ws, 2 * rows), F32),
            pltpu.VMEM((half - 2, pairs, ws), BF16),
            pltpu.VMEM((half - 2, pairs, ws), BF16),
            pltpu.VMEM((half - 2, pairs, ws), BF16),
            pltpu.VMEM((half - 2, pairs, ws), BF16),
            pltpu.VMEM((2, pairs, ws // 2), BF16),
            pltpu.VMEM((2, pairs, ws // 2), BF16),
            pltpu.VMEM((2, pairs, ws), BF16),
            pltpu.VMEM((2, pairs, ws), BF16),
            pltpu.VMEM((sn, high, 128), BF16),
            pltpu.VMEM((sn, high, 128), BF16),
            pltpu.VMEM((sn, high, 128), BF16),
            pltpu.VMEM((sn - 1, high, 128), BF16),
            pltpu.VMEM((2, 4, images), F32),
            dma((5,)),
            dma((2,)),
            dma((2, 2, half)),
            dma((2,)),
            dma((2,)),
            dma((3,)),
            dma((3,)),
            dma((11,)),
            dma((11,)),
        ],
        compiler_params=pltpu.CompilerParams(
            collective_id=0, has_side_effects=True, vmem_limit_bytes=62 * 2**20
        ),
    )(image_student.T, image_teacher, text_student, text_teacher, ss, st)
    loss, grad_image, grad_text = pl.pallas_call(
        deliver,
        out_shape=[jax.ShapeDtypeStruct(v.shape, F32) for v in (loss, grad_image, grad_text)],
        in_specs=[vmem] * 3,
        out_specs=[vmem] * 3,
    )(loss, grad_image, grad_text)
    return loss.reshape(pairs), grad_image.T, grad_text


def solution(mesh):
    zn = mesh.shape["batch"] // 4
    tn = mesh.shape["tensor"]
    return jax.shard_map(
        functools.partial(body, zn, tn),
        mesh=mesh,
        in_specs=(
            P("batch", "tensor"),
            P(("batch", "tensor"), None),
            P("batch", None),
            P(("batch", "tensor"), None),
            P(),
            P(),
        ),
        out_specs=(P(("batch", "tensor")), P("batch", "tensor"), P(("batch", "tensor"), None)),
        check_vma=False,
    )
```

```python
import functools

import jax
import jax.numpy as jnp
from jax import lax
from jax.experimental import pallas as pl
from jax.experimental.pallas import tpu as pltpu
from jax.sharding import PartitionSpec as P

MESH = pl.DeviceIdType.MESH
F32 = jnp.float32
BF16 = jnp.bfloat16
NN = (((1,), (0,)), ((), ()))
NT = (((1,), (1,)), ((), ()))


def remote(src, dst, send, recv, device):
    return pltpu.make_async_remote_copy(
        src_ref=src,
        dst_ref=dst,
        send_sem=send,
        recv_sem=recv,
        device_id=device,
        device_id_type=MESH,
    )


def loop(low, high, body, unroll=False):
    def step(i, carry):
        body(i)
        return carry

    lax.fori_loop(low, high, step, 0, unroll=unroll)


def join_lse(parts):
    peak = functools.reduce(jnp.maximum, parts)
    return peak + jnp.log(sum(jnp.exp(v - peak) for v in parts))


def join_mean(lses, means, lse):
    return sum(jnp.exp(v - lse) * m for v, m in zip(lses, means))


def kernel(
    zn,
    tn,
    xs_ref,
    xt_ref,
    ts_ref,
    tt_ref,
    ss_ref,
    st_ref,
    loss_ref,
    gi_ref,
    gt_ref,
    xs_v,
    buf_a,
    buf_b,
    text_s,
    text_t,
    text_tr,
    stu,
    img_s,
    img_t,
    sc_s,
    sc_t,
    e_rs,
    e_rt,
    e_cs,
    e_ct,
    colstat,
    cbuf,
    cmean,
    rbuf,
    rmean,
    colback,
    g_ref,
    q_ref,
    p_ref,
    dstage,
    dland,
    hstage,
    hland,
    ostage,
    oland,
    fstage,
    fland,
    sstage,
    sland,
    istage,
    iland,
    rsib,
    lsem,
    tsend,
    trecv,
    xsend,
    xrecv,
    ssend,
    srecv,
    send,
    recv,
):
    xn = tn // 2
    half = zn // 2
    b = lax.axis_index("batch")
    t = lax.axis_index("tensor")
    z = lax.div(b, 4)
    ylo = lax.rem(lax.div(b, 2), 2)
    core = lax.rem(b, 2)
    x = lax.div(t, 2)
    yhi = lax.rem(t, 2)
    y = yhi * 2 + ylo
    rb = core * 2 + ylo
    rows = xt_ref.shape[0]
    mid = rows // 2
    pairs, ws = ts_ref.shape
    wt = tt_ref.shape[1]
    wc = (ws + wt) // 2
    wa = wc - ws
    wx = ws // tn
    texts = zn * pairs
    images = 4 * rows
    tile = 2 * pairs

    def at_chip(dx, dy, c):
        x2 = lax.rem(x + dx, xn)
        y2 = lax.rem(y + dy, 4)
        return (4 * z + lax.rem(y2, 2) * 2 + c, x2 * 2 + lax.div(y2, 2))

    def ring(d):
        return (lax.rem(z + d, zn) * 4 + ylo * 2 + core, t)

    sibling = (b + 1 - 2 * core, t)
    right = ring(1)
    left = ring(zn - 1)
    near = [right, left, sibling]
    near += [at_chip(d, 0, core) for d in range(1, xn)]
    near += [at_chip(0, d, core) for d in range(1, 4)]
    barrier = pltpu.get_barrier_semaphore()
    for device in near:
        pl.semaphore_signal(barrier, inc=1, device_id=device, device_id_type=MESH)

    bufs = (buf_a, buf_b)
    texts_in = [
        pltpu.make_async_copy(ts_ref, buf_a.at[z, :, pl.ds(0, ws)], lsem.at[1]),
        pltpu.make_async_copy(
            tt_ref.at[:, pl.ds(0, wa)], buf_a.at[z, :, pl.ds(ws, wa)], lsem.at[2]
        ),
        pltpu.make_async_copy(tt_ref.at[:, pl.ds(wa, wc)], buf_b.at[z], lsem.at[3]),
    ]
    for copy in texts_in:
        copy.start()
    own_xs = pltpu.make_async_copy(xs_ref, xs_v, lsem.at[0])
    own_xs.start()

    def block(r, start, size):
        return img_t.at[pl.ds(pl.multiple_of(r * rows + start, mid), size)]

    own_xt = pltpu.make_async_copy(xt_ref, block(rb, 0, rows), lsem.at[4])
    own_xt.start()

    own_xs.wait()
    whole = xs_v[...].astype(F32)
    odd = ylo == 1
    main = jnp.where(odd, whole[:, rows - 128 :], whole[:, :128])
    rest = jnp.where(odd, whole[:, : rows - 128], whole[:, 128:])
    packed = jnp.concatenate([rest[: wx // 2], rest[wx // 2 :]], 1)

    def stu_place(c, x2, y0, y1):
        return (c * xn + x2) * 4 + y0 * 2 + y1

    own_stu = stu.at[stu_place(core, x, ylo, yhi)]
    own_stu[0:wx, :] = main.astype(BF16)
    own_stu[wx:, :] = packed.astype(BF16)

    for copy in texts_in:
        copy.wait()
    pl.semaphore_wait(barrier, len(near))

    def text_copy(c, way, s):
        o = lax.rem(z + (zn - s if way == 0 else s), zn)
        slot = bufs[c].at[o]
        return remote(
            slot, slot, tsend.at[c], trecv.at[c, way, s], right if way == 0 else left
        )

    def text_wait(c, way, s):
        o = lax.rem(z + (zn - 1 - s if way == 0 else 1 + s), zn)
        slot = bufs[c].at[o]
        remote(slot, slot, tsend.at[c], trecv.at[c, way, s], right).wait_recv()

    def text_step(s):
        for c in range(2):
            for way in range(2):
                if s > half - 1 or (way == 1 and s > half - 2):
                    text_wait(c, way, s - 1)
                else:
                    text_wait(c, way, s - 1)
                    text_copy(c, way, s).start()

    for c in range(2):
        for way in range(2):
            text_copy(c, way, 0).start()

    def stu_y(d):
        return remote(own_stu, own_stu, ssend.at[0], srecv.at[0], at_chip(0, d, core))

    for d in (2, 1, 3):
        stu_y(d).start()

    up = at_chip(0, 1, core)
    down = at_chip(0, 3, core)
    other = core * 2 + 1 - ylo
    far = (1 - core) * 2

    def teach(k, src, dst, device):
        return remote(src, dst, xsend.at[k], xrecv.at[k], device)

    to_up = teach(0, xt_ref.at[pl.ds(0, mid)], block(rb, 0, mid), up)
    to_down = teach(0, xt_ref.at[pl.ds(mid, mid)], block(rb, mid, mid), down)
    to_sib = teach(1, xt_ref, block(rb, 0, rows), sibling)
    to_up.start()
    to_down.start()
    to_sib.start()

    text_step(1)
    def stu_wait(k, count):
        some = stu.at[pl.ds(0, count)]
        remote(some, some, ssend.at[k], srecv.at[k], sibling).wait_recv()

    stu_wait(0, 3)
    own_four = stu.at[pl.ds(stu_place(core, x, 0, 0), 4)]

    def stu_x(d):
        return remote(own_four, own_four, ssend.at[1], srecv.at[1], at_chip(d, 0, core))

    for d in (2, 1, 3):
        stu_x(d).start()
    text_step(2)
    text_step(3)
    sn = 4 * xn
    teach(0, xt_ref, block(other, 0, rows), up).wait_recv()
    to_sib2 = teach(1, block(other, 0, rows), block(other, 0, rows), sibling)
    to_sib2.start()
    stu_wait(1, sn - 4)
    mine = stu.at[pl.ds(core * sn, sn)]
    stu_sib = remote(mine, mine, ssend.at[2], srecv.at[2], sibling)
    stu_sib.start()
    text_step(4)
    own_xt.wait()

    stu_wait(2, sn)
    low = lax.broadcasted_iota(jnp.int32, (wx // 2, 128), 1) < 64

    def unpack(k):
        c = lax.div(k, tn)
        t2 = lax.rem(k, tn)
        even = stu[stu_place(c, lax.div(t2, 2), 0, lax.rem(t2, 2))].astype(F32)
        odds = stu[stu_place(c, lax.div(t2, 2), 1, lax.rem(t2, 2))].astype(F32)
        e2 = even[wx:]
        o2 = odds[wx:]
        middle = jnp.concatenate(
            [jnp.where(low, e2, pltpu.roll(o2, 64, 1)), jnp.where(low, pltpu.roll(e2, 64, 1), o2)],
            0,
        )
        at = pl.ds(pl.multiple_of(t2 * wx, wx), wx)
        for k2, part in enumerate((even[:wx], middle, odds[:wx])):
            lanes = pl.ds(pl.multiple_of(c * 2 * rows + k2 * 128, 128), 128)
            img_s[at, lanes] = part.astype(BF16)

    loop(0, 2 * tn, unpack, True)
    both_far = img_t.at[pl.ds(pl.multiple_of(far * rows, mid), 2 * rows)]
    teach(1, both_far, both_far, sibling).wait_recv()

    factor_s = ss_ref[0] / jnp.sqrt(jnp.float32(ws))
    factor_t = st_ref[0] / jnp.sqrt(jnp.float32(wt))
    lane = lax.broadcasted_iota(jnp.int32, (tile, 128), 1)

    def owners(i):
        more = 1 - lax.div(i, half - 1)
        return lax.rem(z + zn - 1 - i, zn), lax.rem(z + (1 + i) * more, zn)

    def at_owner(o):
        return pl.ds(pl.multiple_of(o * pairs, 8), pairs)

    def fold(v, op):
        out = v[0:8]
        for k in range(1, tile // 8):
            out = op(out, v[8 * k : 8 * k + 8])
        return out

    def batch(first, end):
        last = end == half

        def at_tile(i):
            return pl.ds(pl.multiple_of(i * tile, tile), tile)

        def both(buf, i):
            o1, o2 = owners(i)
            return jnp.concatenate([buf[o1].astype(F32), buf[o2].astype(F32)], 0).astype(BF16)

        def join_a(i):
            one = both(buf_a, i)
            text_s[at_tile(i), :] = one[:, :ws]
            text_t[at_tile(i), pl.ds(0, wa)] = one[:, ws:]

        def join_b(i):
            text_t[at_tile(i), pl.ds(wa, wc)] = both(buf_b, i)

        part = pl.ds(first * tile, (end - first) * tile)

        def teacher(start, size):
            at = pl.ds(start, size)
            return lax.dot_general(
                text_t[part, at], img_t[:, at], NT, preferred_element_type=F32
            )

        if last:
            text_wait(0, 0, half - 1)
        loop(first, end, join_a, True)
        sc_s[part, :] = (
            lax.dot_general(text_s[part, :], img_s[...], NN, preferred_element_type=F32) * factor_s
        )
        if last:
            sc_t[part, :] = teacher(0, wa)
            text_wait(1, 0, half - 1)
        loop(first, end, join_b, True)
        if last:
            sc_t[part, :] = (sc_t[part, :] + teacher(wa, wc)) * factor_t
        else:
            sc_t[part, :] = teacher(0, wt) * factor_t

        def columns(i, carry):
            at = at_tile(i)
            s = sc_s[at, :]
            u = sc_t[at, :]
            ps = jnp.max(s, 1, keepdims=True)
            pt = jnp.max(u, 1, keepdims=True)
            es = jnp.exp(s - ps)
            et = jnp.exp(u - pt)
            e_cs[at, :] = es
            e_ct[at, :] = et
            sums = jnp.sum(es, 1, keepdims=True)
            sumt = jnp.sum(et, 1, keepdims=True)
            mean = jnp.sum(et * s, 1, keepdims=True) / sumt
            out = jnp.where(lane == 0, ps + jnp.log(sums), pt + jnp.log(sumt))
            out = jnp.where(lane == 2, mean, out)
            out = jnp.where(lane == 4, ps, out)
            out = jnp.where(lane == 5, pt, out)
            o1, o2 = owners(i)
            colstat[at_owner(o1), :] = out[:pairs]
            colstat[at_owner(o2), :] = out[pairs:]
            return (
                jnp.maximum(carry[0], fold(s, jnp.maximum)),
                jnp.maximum(carry[1], fold(u, jnp.maximum)),
            )

        none = jnp.full((8, images), -jnp.inf, F32)
        peaks = lax.fori_loop(first, end, columns, (none, none), unroll=True)
        row_ps = jnp.max(peaks[0], 0, keepdims=True)
        row_pt = jnp.max(peaks[1], 0, keepdims=True)

        def by_rows(i, carry):
            at = at_tile(i)
            s = sc_s[at, :]
            es = jnp.exp(s - row_ps)
            et = jnp.exp(sc_t[at, :] - row_pt)
            e_rs[at, :] = es
            e_rt[at, :] = et
            return (
                carry[0] + fold(es, jnp.add),
                carry[1] + fold(et, jnp.add),
                carry[2] + fold(et * s, jnp.add),
            )

        zero = jnp.zeros((8, images), F32)
        sums = lax.fori_loop(first, end, by_rows, (zero, zero, zero), unroll=True)
        return [row_ps, row_pt] + [jnp.sum(v, 0, keepdims=True) for v in sums]

    def ring_place(j):
        return half + (1 - 2 * lax.rem(j, 2)) * lax.div(j + 1, 2)

    def c_copy(j):
        return remote(cbuf.at[zn - 1], cbuf.at[j], send.at[0], recv.at[0], ring(ring_place(j)))

    def cm_copy(j):
        return remote(cmean.at[zn - 1], cmean.at[j], send.at[1], recv.at[1], ring(ring_place(j)))

    def whole_of(buf, k, count):
        some = buf.at[pl.ds(0, count)]
        return remote(some, some, send.at[k], recv.at[k], sibling)

    def send_columns():
        across = colstat[...].T
        cbuf[zn - 1] = across[0:2]
        cmean[zn - 1] = across[2:3]
        loop(0, zn - 1, lambda j: c_copy(j).start(), True)

    cuts = [0, 4, 6, 8]
    text_step(5)
    stats = [batch(0, 4)]
    text_step(6)
    text_step(7)
    stats.append(batch(4, 6))
    stats.append(batch(6, 8))

    def merged(peak, total):
        top = functools.reduce(jnp.maximum, [s[peak] for s in stats])
        scaled = [jnp.exp(s[peak] - top) for s in stats]
        return top, scaled, sum(f * s[total] for f, s in zip(scaled, stats))

    top_s, _, rs = merged(0, 2)
    top_t, scaled, rt = merged(1, 3)
    rw = sum(f * s[4] for f, s in zip(scaled, stats))
    row = lax.broadcasted_iota(jnp.int32, (4, images), 0)

    def rows_of(ls, lt, mean):
        return jnp.where(row == 0, ls, jnp.where(row == 1, lt, mean))

    rsib[0] = rows_of(top_s + jnp.log(rs), top_t + jnp.log(rt), rw / rt)
    r_sib = remote(rsib.at[0], rsib.at[1], send.at[2], recv.at[2], sibling)
    r_sib.start()
    send_columns()
    r_sib.wait_recv()
    chip = [join_lse([rsib[0][k : k + 1], rsib[1][k : k + 1]]) for k in range(2)]
    chip_mean = join_mean(
        [rsib[0][1:2], rsib[1][1:2]], [rsib[0][2:3], rsib[1][2:3]], chip[1]
    )
    rbuf[sn - 1] = rows_of(chip[0], chip[1], chip_mean)[0:2]
    rmean[sn - 1] = chip_mean

    def chip_at(m):
        e = m + lax.div(m, 10)
        return lax.rem(e + 2, 4), lax.rem(lax.div(e, 4) + 2, 4)

    def r_copy(m):
        dx, dy = chip_at(m)
        return remote(rbuf.at[sn - 1], rbuf.at[m], send.at[3], recv.at[3], at_chip(dx, dy, core))

    def rm_copy(m):
        dx, dy = chip_at(m)
        device = at_chip(dx, dy, core)
        return remote(rmean.at[sn - 1], rmean.at[m], send.at[10], recv.at[10], device)

    loop(0, sn - 1, lambda m: r_copy(m).start(), True)
    loop(0, zn - 1, lambda j: cm_copy(j).start(), True)
    loop(0, sn - 1, lambda m: rm_copy(m).start(), True)
    text_tr[...] = text_s[...].astype(F32).T.astype(BF16)

    whole_of(rbuf, 3, sn - 1).wait_recv()
    row_lse = join_lse([rbuf[k] for k in range(sn)])
    whole_of(cbuf, 0, zn - 1).wait_recv()
    col_lse = join_lse([cbuf[k] for k in range(zn)])
    colback[...] = jnp.concatenate([col_lse, jnp.zeros((6, texts), F32)], 0).T

    def grad_tiles(k):
        row_fs = 0.5 * jnp.exp(stats[k][0] - row_lse[0:1])
        row_ft = 0.5 * jnp.exp(stats[k][1] - row_lse[1:2])

        def grads(i, row_fs=row_fs, row_ft=row_ft):
            at = pl.ds(pl.multiple_of(i * tile, tile), tile)
            o1, o2 = owners(i)
            here = jnp.concatenate([colstat[at_owner(o1), :], colstat[at_owner(o2), :]], 0)
            lse = jnp.concatenate([colback[at_owner(o1), :], colback[at_owner(o2), :]], 0)
            fs = 0.5 * jnp.exp(here[:, 4:5] - lse[:, 0:1])
            ft = 0.5 * jnp.exp(here[:, 5:6] - lse[:, 1:2])
            g = e_rs[at, :] * row_fs - e_rt[at, :] * row_ft + e_cs[at, :] * fs - e_ct[at, :] * ft
            g_ref[at, :] = g.astype(BF16)

        loop(cuts[k], cuts[k + 1], grads, True)

    def text_part(first, end):
        at = pl.ds(first * tile, (end - first) * tile)
        part = lax.dot_general(g_ref[at, :], img_s[...], NT, preferred_element_type=F32)
        q_ref[2 * first : 2 * end] = part.reshape(2 * (end - first), pairs, ws)


    def place(way, d):
        return 2 * (half - 1) if d == half else 2 * (d - 1) + (1 if way == 0 else 0)

    def hop(way, d):
        return ring(d % zn if way == 0 else (zn - d) % zn)

    quarter = half // 2
    relays = [(w, d) for d in range(quarter - 1, 0, -1) for w in range(2)] + [(0, -1), (1, -1)]
    directs = [(w, d) for d in range(quarter - 2, 0, -1) for w in range(2)]
    wg = ws // 2

    def h_copy(k):
        return remote(hstage.at[k], hland.at[k], send.at[4], recv.at[4], hop(*relays[k]))

    def d_copy(k):
        return remote(dstage.at[k], dland.at[k], send.at[5], recv.at[5], hop(*directs[k]))

    def o_copy(way):
        return remote(
            ostage.at[way], oland.at[way], send.at[9], recv.at[9], hop(way, quarter)
        )

    def f_copy(way):
        return remote(
            fstage.at[way], fland.at[way], send.at[6], recv.at[6], hop(way, quarter)
        )

    grad_tiles(1)
    grad_tiles(2)
    text_part(quarter, half)
    for way in range(2):
        ostage[way] = q_ref[place(way, half), :, way * wg : (way + 1) * wg].astype(BF16)
        o_copy(way).start()
    def to_relay(k):
        way, d = relays[k]
        hstage[k] = q_ref[place(way, d + quarter)].astype(BF16)
        h_copy(k).start()

    for k in range(len(relays) - 2):
        to_relay(k)
    grad_tiles(0)


    def image_part(c):
        at = pl.ds(pl.multiple_of(c * 2 * rows, 128), 2 * rows)
        p_ref[...] = jnp.dot(text_tr[...], g_ref[:, at], preferred_element_type=F32)

    def pack(out, more, t2):
        at = pl.ds(pl.multiple_of(t2 * wx, wx), wx)
        middle = p_ref[at, 128:256]
        m1 = middle[: wx // 2]
        m2 = middle[wx // 2 :]
        parts = (
            (p_ref[at, 0:128], jnp.where(low, m1, pltpu.roll(m2, 64, 1))),
            (p_ref[at, 256:384], jnp.where(low, pltpu.roll(m1, 64, 1), m2)),
        )
        for y0, (main, rest) in enumerate(parts):
            k = stu_place(0, lax.div(t2, 2), y0, lax.rem(t2, 2))
            if more is not None:
                main = main + more[k, pl.ds(0, wx), :].astype(F32)
                rest = rest + more[k, pl.ds(wx, wx // 2), :].astype(F32)
            out[k, pl.ds(0, wx), :] = main.astype(BF16)
            out[k, pl.ds(wx, wx // 2), :] = rest.astype(BF16)

    image_part(1 - core)
    loop(0, tn, lambda t2: pack(sstage, None, t2), True)
    i_sib = remote(sstage, sland, send.at[7], recv.at[7], sibling)
    i_sib.start()
    text_part(0, quarter)
    to_relay(len(relays) - 2)
    to_relay(len(relays) - 1)
    for k, (way, d) in enumerate(directs):
        dstage[k] = q_ref[place(way, d)].astype(BF16)
        d_copy(k).start()
    image_part(core)
    i_sib.wait_recv()
    loop(0, tn, lambda t2: pack(istage, sland, t2), True)

    def i_copy(m):
        dx, dy = chip_at(m)
        y2 = lax.rem(y + dy, 4)
        src = istage.at[
            stu_place(0, lax.rem(x + dx, xn), lax.rem(y2, 2), lax.div(y2, 2))
        ]
        return remote(src, iland.at[m], send.at[8], recv.at[8], at_chip(dx, dy, core))

    loop(0, sn - 1, lambda m: i_copy(m).start(), True)

    whole_of(hland, 4, len(relays)).wait_recv()
    whole_of(oland, 9, 2).wait_recv()
    for way in range(2):
        total = q_ref[place(way, quarter)]
        for k, (w, d) in enumerate(relays):
            if w == way:
                total = total + hland[k].astype(F32)
        farthest = oland[way].astype(F32)
        zero = jnp.zeros((pairs, wg), F32)
        total = total + jnp.concatenate([farthest, zero] if way == 0 else [zero, farthest], 1)
        fstage[way] = total.astype(BF16)
        f_copy(way).start()

    whole_of(cmean, 1, zn - 1).wait_recv()
    whole_of(rmean, 10, sn - 1).wait_recv()
    col_mean = join_mean(
        [cbuf[k][1:2] for k in range(zn)], [cmean[k] for k in range(zn)], col_lse[1:2]
    )
    row_mean = join_mean(
        [rbuf[k][1:2] for k in range(sn)], [rmean[k] for k in range(sn)], row_lse[1:2]
    )
    col_loss = col_lse[0:1] - col_mean
    row_loss = row_lse[0:1] - row_mean
    own_col = pltpu.roll(jnp.broadcast_to(col_loss, (8, texts)), texts - z * pairs, 1)
    own_row = pltpu.roll(
        jnp.broadcast_to(row_loss, (8, images)), images - rb * rows - t * pairs, 1
    )
    loss_ref[...] = 0.5 * (own_col[0:1, 0:pairs] + own_row[0:1, 0:pairs])

    for c in range(2):
        some = bufs[c].at[pl.ds(0, zn - 1)]
        remote(some, some, tsend.at[c], trecv.at[c, 0, 0], sibling).wait_send()
    for k, count in ((0, 3), (1, 12), (2, sn)):
        some = stu.at[pl.ds(0, count)]
        remote(some, some, ssend.at[k], srecv.at[k], sibling).wait_send()
    teach(0, xt_ref, block(rb, 0, rows), sibling).wait_send()
    teach(1, both_far, both_far, sibling).wait_send()
    whole_of(cbuf, 0, zn - 1).wait_send()
    whole_of(cmean, 1, zn - 1).wait_send()
    r_sib.wait_send()
    whole_of(rbuf, 3, sn - 1).wait_send()
    whole_of(rmean, 10, sn - 1).wait_send()
    whole_of(hstage, 4, len(relays)).wait_send()
    whole_of(ostage, 9, 2).wait_send()
    whole_of(dstage, 5, len(directs)).wait_send()
    i_sib.wait_send()

    whole_of(iland, 8, sn - 1).wait_recv()
    total = istage[stu_place(0, x, ylo, yhi)].astype(F32)
    for k in range(sn - 1):
        total = total + iland[k].astype(F32)
    total = total * factor_s
    main = total[:wx]
    rest = jnp.concatenate([total[wx:, :64], total[wx:, 64:]], 0)
    gi_ref[...] = jnp.where(
        odd, jnp.concatenate([rest, main], 1), jnp.concatenate([main, rest], 1)
    )
    whole_of(iland, 8, sn - 1).wait_send()

    whole_of(dland, 5, len(directs)).wait_recv()
    total = q_ref[zn - 1]
    for k in range(len(directs)):
        total = total + dland[k].astype(F32)
    whole_of(fland, 6, 2).wait_recv()
    for way in range(2):
        total = total + fland[way].astype(F32)
    gt_ref[...] = total * factor_s
    whole_of(fland, 6, 2).wait_send()


def deliver(loss_ref, image_ref, text_ref, loss_out, image_out, text_out):
    loss_out[...] = loss_ref[...]
    image_out[...] = image_ref[...]
    text_out[...] = text_ref[...]


def body(zn, tn, image_student, text_student, image_teacher, text_teacher, ss, st):
    rows = image_teacher.shape[0]
    pairs, ws = text_student.shape
    wt = text_teacher.shape[1]
    wx = ws // tn
    texts, images, half = zn * pairs, 4 * rows, zn // 2
    sn = 2 * tn
    high = wx * rows // 128
    dma = pltpu.SemaphoreType.DMA
    anywhere = pl.BlockSpec(memory_space=pl.ANY)
    vmem = pl.BlockSpec(memory_space=pltpu.VMEM)
    smem = pl.BlockSpec(memory_space=pltpu.SMEM)
    score = pltpu.VMEM((texts, images), F32)
    loss, grad_image, grad_text = pl.pallas_call(
        functools.partial(kernel, zn, tn),
        out_shape=(
            jax.ShapeDtypeStruct((1, pairs), F32),
            jax.ShapeDtypeStruct((wx, rows), F32),
            jax.ShapeDtypeStruct((pairs, ws), F32),
        ),
        in_specs=[anywhere] * 4 + [smem, smem],
        out_specs=(vmem, vmem, vmem),
        scratch_shapes=[
            pltpu.VMEM((wx, rows), BF16),
            pltpu.VMEM((zn, pairs, (ws + wt) // 2), BF16),
            pltpu.VMEM((zn, pairs, (ws + wt) // 2), BF16),
            pltpu.VMEM((texts, ws), BF16),
            pltpu.VMEM((texts, wt), BF16),
            pltpu.VMEM((ws, texts), BF16),
            pltpu.VMEM((2 * sn, high, 128), BF16),
            pltpu.VMEM((ws, images), BF16),
            pltpu.VMEM((images, wt), BF16),
            score,
            score,
            score,
            score,
            score,
            score,
            pltpu.VMEM((texts, 128), F32),
            pltpu.VMEM((zn, 2, texts), F32),
            pltpu.VMEM((zn, 1, texts), F32),
            pltpu.VMEM((sn, 2, images), F32),
            pltpu.VMEM((sn, 1, images), F32),
            pltpu.VMEM((texts, 8), F32),
            pltpu.VMEM((texts, images), BF16),
            pltpu.VMEM((zn, pairs, ws), F32),
            pltpu.VMEM((ws, 2 * rows), F32),
            pltpu.VMEM((half - 4, pairs, ws), BF16),
            pltpu.VMEM((half - 4, pairs, ws), BF16),
            pltpu.VMEM((half, pairs, ws), BF16),
            pltpu.VMEM((half, pairs, ws), BF16),
            pltpu.VMEM((2, pairs, ws // 2), BF16),
            pltpu.VMEM((2, pairs, ws // 2), BF16),
            pltpu.VMEM((2, pairs, ws), BF16),
            pltpu.VMEM((2, pairs, ws), BF16),
            pltpu.VMEM((sn, high, 128), BF16),
            pltpu.VMEM((sn, high, 128), BF16),
            pltpu.VMEM((sn, high, 128), BF16),
            pltpu.VMEM((sn - 1, high, 128), BF16),
            pltpu.VMEM((2, 4, images), F32),
            dma((5,)),
            dma((2,)),
            dma((2, 2, half)),
            dma((2,)),
            dma((2,)),
            dma((3,)),
            dma((3,)),
            dma((11,)),
            dma((11,)),
        ],
        compiler_params=pltpu.CompilerParams(
            collective_id=0, has_side_effects=True, vmem_limit_bytes=62 * 2**20
        ),
    )(image_student.T, image_teacher, text_student, text_teacher, ss, st)
    loss, grad_image, grad_text = pl.pallas_call(
        deliver,
        out_shape=[jax.ShapeDtypeStruct(v.shape, F32) for v in (loss, grad_image, grad_text)],
        in_specs=[vmem] * 3,
        out_specs=[vmem] * 3,
    )(loss, grad_image, grad_text)
    return loss.reshape(pairs), grad_image.T, grad_text


def solution(mesh):
    zn = mesh.shape["batch"] // 4
    tn = mesh.shape["tensor"]
    return jax.shard_map(
        functools.partial(body, zn, tn),
        mesh=mesh,
        in_specs=(
            P("batch", "tensor"),
            P(("batch", "tensor"), None),
            P("batch", None),
            P(("batch", "tensor"), None),
            P(),
            P(),
        ),
        out_specs=(P(("batch", "tensor")), P("batch", "tensor"), P(("batch", "tensor"), None)),
        check_vma=False,
    )
```
